256 devices in a mesh: ctx: 16 (over z, core), ch: 4 (over x), dp: 4 (over y).
Axes of the slice: x: 4, y: 4, z: 8, core: 2. Of those that a mesh axis runs over, the one named last changes fastest.
Arguments:
- query_rows: bfloat16 [4, 2048, 8192], P('dp', 'ctx', 'ch'), may hold values from -6 to 6
- key_rows: bfloat16 [4, 2048, 8192], P('dp', 'ctx', 'ch'), may hold values from -6 to 6
- value_rows: bfloat16 [4, 2048, 8192], P('dp', 'ctx', 'ch'), may hold values from -6 to 6
- cotangent: bfloat16 [4, 2048, 8192], P('dp', 'ctx', 'ch'), may hold values from -6 to 6
- lengths: int32 [4, 8], P('dp'), may hold values from 1 to 1024, 2048 in all within a row
- short_filter: float32 [3, 7, 8192], P(None, None, 'ch'), may hold values from -2.5 to 2.5
- residue: float32 [8192, 16], P('ch'), may hold values from -1.5 to 1.5
- decay_rate: float32 [8192, 16], P('ch'), may hold values from 0.00024414062 to 0.0625
- skip_gain: float32 [8192], P('ch'), may hold values from 0.5 to 1.5
Outputs:
- block_out: bfloat16 [4, 2048, 8192], P('dp', 'ctx', 'ch')
- grad_query: bfloat16 [4, 2048, 8192], P('dp', 'ctx', 'ch')
- grad_key: bfloat16 [4, 2048, 8192], P('dp', 'ctx', 'ch')
- grad_value: bfloat16 [4, 2048, 8192], P('dp', 'ctx', 'ch')
- grad_short: float32 [3, 7, 8192], P(None, None, 'ch')
- grad_residue: float32 [8192, 16], P('ch')
- grad_skip: float32 [8192], P('ch')
The draws below stay inside these ranges and needn't reach their ends.
Inputs may be any that keep to these rules, and one draw needn't show every extreme that they name: Each row of lengths sums to 2048, and its longest document holds exactly 1024 positions.
All inputs are finite; a program needn't handle non-finite values.
Results may differ from the reference program's by a relative error of at most 0.0011.
Values may be sent and summed in bfloat16 or wider, within the bound.
No kernel may reach another device: no remote copies, remote signals or barrier semaphores. Data moves between devices by JAX's collectives and lax.ppermute only.
A program may use at most 128 MiB of HBM per device.

```python
import math
from functools import partial
import jax
import jax.numpy as jnp
import numpy as np
from jax import lax

D = 8192
MODES = 16
TAPS = 7
DOCS = 8
TOK_DEV = 128
SEQ = 2048
BATCH = 4
N_CTX = 16


def levels(rng, shape, shards, low, top_value):
    gain, own = 1.0, jax.random.fold_in(rng, 6)
    for dim, blocks in shards:
        heights = jnp.exp(jax.random.uniform(jax.random.fold_in(own, dim), (blocks,), jnp.float32, low / len(shards), top_value / len(shards)))
        gain = gain * jnp.repeat(heights, shape[dim] // blocks).reshape([-1 if axis == dim else 1 for axis in range(len(shape))])
    return gain


def length_profile(count, total, limit, slope):
    portions = [(1 << 20) // math.isqrt(grade ** slope) + 1 for grade in range(2, count + 1)]
    rest, counts = total - limit - (count - 1), [1] * (count - 1)
    while rest > 0:
        free = [i for i in range(count - 1) if counts[i] < limit]
        pool, budget = sum([portions[i] for i in free]), rest
        for i in free:
            extra = min(limit - counts[i], max(1, budget * portions[i] // pool), rest)
            counts[i] = counts[i] + extra
            rest = rest - extra
    return np.array([limit] + counts)


def uneven_parts(key, number_of, total, most, lean):
    if number_of == 2:
        one = jax.random.randint(key, (), max(1, total - most), min(most, total - 1) + 1)
        return jnp.stack([one, total - one])
    sizes = jnp.asarray(length_profile(number_of, total, most, lean), jnp.int32)
    couples = (number_of - 1) // 2
    giver, receiver = sizes[1:1 + 2 * couples:2], sizes[2:2 + 2 * couples:2]
    margin = jnp.minimum(giver - 1, most - receiver)
    passed = jax.random.randint(jax.random.fold_in(key, 1), (couples,), 0, 1 << 20) % (margin + 1)
    sizes = sizes.at[1:1 + 2 * couples:2].set(giver - passed).at[2:2 + 2 * couples:2].set(receiver + passed)
    return sizes[jax.random.permutation(jax.random.fold_in(key, 2), number_of)]


def gaussian(key, shape, spread, bound, cuts=(), kind=jnp.bfloat16):
    gain = levels(key, shape, cuts, -0.22, 0.18) if cuts else 1.0
    array = jax.random.normal(key, shape, jnp.float32) * spread * gain
    return jnp.minimum(jnp.maximum(array, -bound), bound).astype(kind)


def setup_inputs(seed: int = 0) -> dict:
    arg_keys = jax.random.split(jax.random.key(seed), 10)
    query_rows = gaussian(arg_keys[0], (BATCH, SEQ, D), 1.0, 6.0, ((0, 4), (1, 16), (2, 4)))
    key_rows = gaussian(arg_keys[1], (BATCH, SEQ, D), 1.0, 6.0, ((0, 4), (1, 16), (2, 4)))
    value_rows = gaussian(arg_keys[2], (BATCH, SEQ, D), 1.0, 6.0, ((0, 4), (1, 16), (2, 4)))
    cotangent = gaussian(arg_keys[3], (BATCH, SEQ, D), 1.0, 6.0, ((0, 4), (1, 16), (2, 4)))
    lengths = jax.vmap(lambda own: uneven_parts(own, DOCS, SEQ, SEQ // 2, 2))(jax.random.split(arg_keys[4], BATCH)).reshape((BATCH, DOCS)).astype(jnp.int32)
    short_filter = gaussian(arg_keys[5], (3, TAPS, D), 0.4, 2.5, ((2, 4),), jnp.float32)
    residue = gaussian(arg_keys[6], (D, MODES), MODES ** -0.5, 1.5, ((0, 4),), jnp.float32)
    decay_rate = jnp.clip(jnp.exp(math.log(0.0625) - 5.5451774 * jax.random.uniform(arg_keys[7], (D, MODES), jnp.float32) ** levels(arg_keys[7], (D, MODES), ((0, 4),), -0.2, 0.2)), 0.00024414062, 0.0625)
    skip_gain = jnp.clip(0.5 + 1.0 * jax.random.uniform(arg_keys[8], (D,), jnp.float32) ** levels(arg_keys[8], (D,), ((0, 4),), -0.2, 0.2), 0.5, 1.5)
    return {"query_rows": query_rows, "key_rows": key_rows, "value_rows": value_rows, "cotangent": cotangent, "lengths": lengths, "short_filter": short_filter, "residue": residue, "decay_rate": decay_rate, "skip_gain": skip_gain}


def short_conv(source, filters, doc_rows):
    summed = jnp.zeros_like(source)
    for shift_by in range(TAPS):
        shifted = jnp.pad(source, ((shift_by, 0), (0, 0)))[:SEQ]
        shifted_docs = jnp.pad(doc_rows, (shift_by, 0), constant_values=-1)[:SEQ]
        kept_rows = (shifted_docs == doc_rows).astype(jnp.float32)
        summed = summed + filters[shift_by][None, :] * shifted * kept_rows[:, None]
    return summed

def long_conv(source, weight, decay_step, fresh_rows):

    def advance(state_now, inputs):
        column, restart = inputs
        state_now = decay_step * state_now * (1.0 - restart) + column[:, None]
        return (state_now, lax.optimization_barrier(jnp.sum(state_now * weight, axis=1)))

    def block_fn(state_now, inputs):
        return lax.scan(advance, state_now, inputs)
    blocked = (source.reshape(N_CTX, TOK_DEV, D), fresh_rows.reshape(N_CTX, TOK_DEV))
    initial = jnp.zeros((D, MODES), jnp.float32)
    unused, outputs = lax.scan(jax.checkpoint(block_fn), initial, blocked)
    return outputs.reshape(SEQ, D)

def forward(query_in, key_in, value_in, filters, residues, gains, doc_rows, fresh_rows, rates):
    query_feat = short_conv(query_in, filters[0], doc_rows)
    key_feat = short_conv(key_in, filters[1], doc_rows)
    value_feat = short_conv(value_in, filters[2], doc_rows)
    product = key_feat * value_feat
    weight = residues * jnp.sqrt(rates)
    filtered = long_conv(product, weight, jnp.exp(-rates), fresh_rows) + gains[None, :] * product
    return query_feat * filtered

def reference(query_rows, key_rows, value_rows, cotangent, lengths, short_filter, residue, decay_rate, skip_gain):
    positions = jnp.arange(SEQ, dtype=jnp.int32)
    out_list, gq_list, gk_list, gv_list = ([], [], [], [])
    grad_short = jnp.zeros(short_filter.shape, jnp.float32)
    grad_residue = jnp.zeros(residue.shape, jnp.float32)
    grad_skip = jnp.zeros(skip_gain.shape, jnp.float32)
    for batch_row in range(BATCH):
        doc_lengths = lengths[batch_row]
        starts = jnp.cumsum(doc_lengths) - doc_lengths
        doc_rows = lax.optimization_barrier(jnp.sum((positions[:, None] >= starts[None, :]).astype(jnp.int32), axis=1))
        fresh_rows = lax.optimization_barrier(jnp.sum((positions[:, None] == starts[None, :]).astype(jnp.float32), axis=1))
        bound_fn = partial(forward, doc_rows=doc_rows, fresh_rows=fresh_rows, rates=decay_rate)
        primal, pullback = jax.vjp(bound_fn, query_rows[batch_row].astype(jnp.float32), key_rows[batch_row].astype(jnp.float32), value_rows[batch_row].astype(jnp.float32), short_filter, residue, skip_gain)
        grads = pullback(cotangent[batch_row].astype(jnp.float32))
        out_list.append(primal.astype(jnp.bfloat16))
        gq_list.append(grads[0].astype(jnp.bfloat16))
        gk_list.append(grads[1].astype(jnp.bfloat16))
        gv_list.append(grads[2].astype(jnp.bfloat16))
        grad_short = grad_short + grads[3]
        grad_residue = grad_residue + grads[4]
        grad_skip = grad_skip + grads[5]
    return (jnp.stack(out_list), jnp.stack(gq_list), jnp.stack(gk_list), jnp.stack(gv_list), grad_short, grad_residue, grad_skip)
```

```python
import jax
import jax.numpy as jnp
from jax import lax
from jax.experimental import pallas as pl
from jax.experimental.pallas import tpu as pltpu
from jax.sharding import PartitionSpec as P

SEGS = 8
STEPS = 16
ROWS = SEGS * STEPS
TAPS = 7
HALO = TAPS - 1
MODES = 16
LANES = 128
REDUCED = 40
F32 = jnp.float32
VMEM_BYTES = 56 << 20


def lanes_of(tile):
    return pl.ds(pl.multiple_of(tile * LANES, LANES), LANES)


def row(ref, index, lanes):
    return jnp.broadcast_to(ref[index : index + 1, lanes], (SEGS, LANES))


def slab(index):
    return slice(index * SEGS, (index + 1) * SEGS)


def store_masks(dist_ref, mask_ref, steps, gaps):
    for gap in range(1, gaps + 1):
        for t in range(steps):
            mask_ref[gap - 1, t] = (dist_ref[t] >= gap).astype(F32)


def fetch_columns(ref, stage, lanes):
    stage[...] = ref[:, lanes].astype(F32)
    return [stage[pl.ds(t, SEGS, stride=STEPS), :] for t in range(STEPS)]


def feature_kernel(
    q_ref, k_ref, v_ref, cot_ref, halo_ref, taps_ref, decay_ref, dist_ref, end_ref, chain_ref,
    raw_ref, feat_ref, cot_out, source_ref, grad_ref, gseg_ref, sloc_ref, rloc_ref, end_out, begin_out,
    stage, masks, open_mask, end_mask,
):
    store_masks(dist_ref, masks, STEPS, HALO)
    for t in range(STEPS):
        open_mask[t] = (dist_ref[t] >= t + 1).astype(F32)
        end_mask[t] = (end_ref[...] >= STEPS - 1 - t).astype(F32)

    def tile_body(tile, carry):
        lanes = lanes_of(tile)
        segment = lax.broadcasted_iota(jnp.int32, (SEGS, LANES), 0)
        first, last = segment == 0, segment == SEGS - 1
        for branch, ref in enumerate((q_ref, k_ref, v_ref)):
            rows = fetch_columns(ref, stage.at[branch], lanes)
            before = {}
            for back in range(1, HALO + 1):
                edge = row(halo_ref, branch * 8 + 8 - back, lanes)
                before[-back] = jnp.where(first, edge, pltpu.roll(rows[STEPS - back], 1, 0))
            taps = [row(taps_ref, branch * TAPS + j, lanes) for j in range(TAPS)]
            for t in range(STEPS):
                raw_ref[branch, slab(t), lanes] = rows[t]
                total = taps[0] * rows[t]
                for j in range(1, TAPS):
                    earlier = rows[t - j] if t >= j else before[t - j]
                    total = total + taps[j] * (earlier * masks[j - 1, t])
                feat_ref[branch, slab(t), lanes] = total
        upstream = fetch_columns(cot_ref, stage.at[3], lanes)
        for t in range(STEPS):
            cot_out[slab(t), lanes] = upstream[t]
            source_ref[slab(t), lanes] = feat_ref[1, slab(t), lanes] * feat_ref[2, slab(t), lanes]
            grad_ref[slab(t), lanes] = upstream[t] * feat_ref[0, slab(t), lanes]
        for low in range(0, MODES, 8):
            modes = range(low, low + 8)
            decay = [row(decay_ref, m, lanes) for m in modes]
            ends = [source_ref[slab(0), lanes] * end_mask[0]] * 8
            for t in range(1, STEPS):
                value = source_ref[slab(t), lanes] * end_mask[t]
                ends = [d * e + value for d, e in zip(decay, ends)]
            begins = [grad_ref[slab(STEPS - 1), lanes] * open_mask[STEPS - 1]] * 8
            for t in range(STEPS - 2, -1, -1):
                value = grad_ref[slab(t), lanes] * open_mask[t]
                begins = [d * b + value for d, b in zip(decay, begins)]
            for m, d, e, b in zip(modes, decay, ends, begins):
                gseg_ref[slab(m), lanes] = b
                for _ in range(4):
                    d = d * d
                for k in range(3):
                    e = e + (d * chain_ref[k]) * pltpu.roll(e, 1 << k, 0)
                    b = b + (d * chain_ref[3 + k]) * pltpu.roll(b, SEGS - (1 << k), 0)
                    d = d * d
                sloc_ref[slab(m), lanes] = jnp.where(first, 0.0, pltpu.roll(e, 1, 0))
                rloc_ref[slab(m), lanes] = jnp.where(last, 0.0, pltpu.roll(b, SEGS - 1, 0))
                end_out[m : m + 1, lanes] = e[SEGS - 1 :]
                begin_out[m : m + 1, lanes] = b[:1]
        return carry

    lax.fori_loop(0, q_ref.shape[1] // LANES, tile_body, 0)


def local_kernel(
    source_ref, grad_ref, gseg_ref, sloc_ref, rloc_ref, decay_ref, rate_ref, weight_ref, skip_ref, dist_ref, reach_ref,
    conv_ref, back_ref, swt_ref, rwt_ref, scoef_ref, rcoef_ref, local_ref,
    masks, stage,
):
    store_masks(dist_ref, masks, STEPS, STEPS - 1)

    def tile_body(tile, carry):
        lanes = lanes_of(tile)
        segment = lax.broadcasted_iota(jnp.int32, (SEGS, LANES), 0).astype(F32)
        decay = decay_ref[:, lanes]
        power = weight_ref[:, lanes]
        kernel = []
        for gap in range(STEPS):
            kernel.append(jnp.sum(power, axis=0, keepdims=True))
            power = power * decay
        kernel[0] = kernel[0] + skip_ref[:, lanes]
        source = [source_ref[slab(t), lanes] for t in range(STEPS)]
        grads = [grad_ref[slab(t), lanes] for t in range(STEPS)]
        conv, back, paired = [None] * STEPS, [None] * STEPS, []
        for gap in range(STEPS):
            weight = jnp.broadcast_to(kernel[gap], (SEGS, LANES))
            pair = jnp.zeros((SEGS, LANES), F32)
            for t in range(gap, STEPS):
                value, grad = source[t - gap], grads[t]
                if gap:
                    value, grad = value * masks[gap - 1, t], grad * masks[gap - 1, t]
                conv[t] = weight * value if gap == 0 else conv[t] + weight * value
                back[t - gap] = weight * grad if gap == 0 else back[t - gap] + weight * grad
                pair = pair + grads[t] * value
            paired.append(jnp.sum(pair, axis=0, keepdims=True))
        for t in range(STEPS):
            conv_ref[slab(t), lanes] = conv[t]
            back_ref[slab(t), lanes] = back[t]
        total = jnp.broadcast_to(paired[STEPS - 1], (MODES, LANES))
        for gap in range(STEPS - 2, -1, -1):
            total = total * decay + paired[gap]
        for m in range(MODES):
            arriving = sloc_ref[slab(m), lanes]
            stage[m : m + 1, :] = jnp.sum(arriving * gseg_ref[slab(m), lanes], axis=0, keepdims=True)
            scale = row(weight_ref, m, lanes) * row(decay_ref, m, lanes)
            rate = row(rate_ref, m, lanes) * (-float(STEPS))
            swt_ref[slab(m), lanes] = scale * arriving
            rwt_ref[slab(m), lanes] = scale * rloc_ref[slab(m), lanes]
            scoef_ref[slab(m), lanes] = scale * reach_ref[0] * jnp.exp(rate * segment)
            rcoef_ref[slab(m), lanes] = scale * reach_ref[1] * jnp.exp(rate * (SEGS - 1 - segment))
        local_ref[tile, 0:MODES] = total + stage[...] * decay
        local_ref[tile, MODES : MODES + 8] = jnp.broadcast_to(paired[0], (8, LANES))
        return carry

    lax.fori_loop(0, decay_ref.shape[1] // LANES, tile_body, 0)


def gradient_kernel(
    raw_ref, feat_ref, cot_ref, conv_ref, back_ref, swt_ref, rwt_ref, scoef_ref, rcoef_ref, local_ref,
    enter_ref, return_ref, begin_ref, decay_ref, root_ref, halo_ref, dist_ref, end_ref,
    out_ref, gfeat_ref, edge_ref, reduced_ref,
    stage, masks, open_mask, end_mask,
):
    store_masks(dist_ref, masks, STEPS, HALO)
    for t in range(STEPS):
        open_mask[t] = (dist_ref[t] >= t + 1).astype(F32)
        end_mask[t] = (end_ref[...] >= STEPS - 1 - t).astype(F32)

    def tile_body(tile, carry):
        lanes = lanes_of(tile)
        segment = lax.broadcasted_iota(jnp.int32, (SEGS, LANES), 0)
        first = segment == 0
        decay = [row(decay_ref, m, lanes) for m in range(MODES)]
        state = [
            swt_ref[slab(m), lanes] + scoef_ref[slab(m), lanes] * row(enter_ref, m, lanes)
            for m in range(MODES)
        ]
        for t in range(STEPS):
            filtered = conv_ref[slab(t), lanes] + open_mask[t] * tree_sum(state)
            stage[pl.ds(t, SEGS, stride=STEPS), :] = feat_ref[0, slab(t), lanes] * filtered
            gfeat_ref[0, slab(t), lanes] = cot_ref[slab(t), lanes] * filtered
            if t < STEPS - 1:
                state = [d * s for d, s in zip(decay, state)]
        out_ref[:, lanes] = stage[...].astype(out_ref.dtype)
        state = [
            rwt_ref[slab(m), lanes] + rcoef_ref[slab(m), lanes] * row(return_ref, m, lanes)
            for m in range(MODES)
        ]
        for t in range(STEPS - 1, -1, -1):
            grad = back_ref[slab(t), lanes] + end_mask[t] * tree_sum(state)
            gfeat_ref[1, slab(t), lanes] = grad * feat_ref[2, slab(t), lanes]
            gfeat_ref[2, slab(t), lanes] = grad * feat_ref[1, slab(t), lanes]
            if t:
                state = [d * s for d, s in zip(decay, state)]
        reduced_ref[tile, 0:MODES] = root_ref[:, lanes] * (
            local_ref[tile, 0:MODES] + enter_ref[:, lanes] * decay_ref[:, lanes] * begin_ref[:, lanes]
        )
        for branch in range(3):
            totals = [jnp.zeros((SEGS, LANES), F32)] * TAPS
            rows = [raw_ref[branch, slab(t), lanes] for t in range(STEPS)]
            before = {}
            for back in range(1, HALO + 1):
                edge = row(halo_ref, branch * 8 + 8 - back, lanes)
                before[-back] = jnp.where(first, edge, pltpu.roll(rows[STEPS - back], 1, 0))
            for t in range(STEPS):
                grad = gfeat_ref[branch, slab(t), lanes]
                if t < HALO:
                    edge_ref[branch * 8 + t : branch * 8 + t + 1, lanes] = grad[:1]
                totals[0] = totals[0] + grad * rows[t]
                for j in range(1, TAPS):
                    earlier = rows[t - j] if t >= j else before[t - j]
                    totals[j] = totals[j] + (grad * masks[j - 1, t]) * earlier
            edge_ref[branch * 8 + HALO : branch * 8 + 8, lanes] = jnp.zeros((8 - HALO, LANES), F32)
            for j in range(TAPS):
                at = MODES + branch * TAPS + j
                reduced_ref[tile, at : at + 1] = jnp.sum(totals[j], axis=0, keepdims=True)
        at = MODES + 3 * TAPS
        reduced_ref[tile, at:REDUCED] = local_ref[tile, MODES : MODES + REDUCED - at]
        return carry

    lax.fori_loop(0, decay_ref.shape[1] // LANES, tile_body, 0)


def tree_sum(values):
    while len(values) > 1:
        values = [a + b for a, b in zip(values[::2], values[1::2])]
    return values[0]


def input_kernel(gfeat_ref, edge_ref, taps_ref, dist_ref, gq_ref, gk_ref, gv_ref, stage, masks):
    store_masks(dist_ref, masks, STEPS + HALO, HALO)

    def tile_body(tile, carry):
        lanes = lanes_of(tile)
        segment = lax.broadcasted_iota(jnp.int32, (SEGS, LANES), 0)
        last = segment == SEGS - 1
        for branch, out_ref in enumerate((gq_ref, gk_ref, gv_ref)):
            rows = [gfeat_ref[branch, slab(t), lanes] for t in range(STEPS)]
            for t in range(HALO):
                edge = row(edge_ref, branch * 8 + t, lanes)
                rows.append(jnp.where(last, edge, pltpu.roll(rows[t], SEGS - 1, 0)))
            taps = [row(taps_ref, branch * TAPS + j, lanes) for j in range(TAPS)]
            for t in range(STEPS):
                total = taps[0] * rows[t]
                for j in range(1, TAPS):
                    total = total + taps[j] * (rows[t + j] * masks[j - 1, t + j])
                stage[branch, pl.ds(t, SEGS, stride=STEPS), :] = total
            out_ref[:, lanes] = stage[branch].astype(out_ref.dtype)
        return carry

    lax.fori_loop(0, gq_ref.shape[1] // LANES, tile_body, 0)


def call(body, name, outs, scratch, flops, *args):
    return pl.pallas_call(
        body,
        name=name,
        out_shape=[jax.ShapeDtypeStruct(shape, dtype) for shape, dtype in outs],
        in_specs=[pl.BlockSpec(memory_space=pltpu.VMEM)] * len(args),
        out_specs=[pl.BlockSpec(memory_space=pltpu.VMEM)] * len(outs),
        scratch_shapes=[pltpu.VMEM(shape, F32) for shape in scratch],
        compiler_params=pltpu.CompilerParams(vmem_limit_bytes=VMEM_BYTES),
        cost_estimate=pl.CostEstimate(flops=flops, bytes_accessed=8 << 20, transcendentals=0),
    )(*args)


def per_device(query_rows, key_rows, value_rows, cotangent, lengths, short_filter, residue, decay_rate, skip_gain):
    channels = query_rows.shape[2]
    tiles = channels // LANES
    count = lax.axis_size("ctx")
    here = lax.axis_index("ctx")
    chip, core = here // 2, here % 2
    anchor = here * ROWS

    order = jnp.arange(lengths.shape[1])
    starts = jnp.sum(jnp.where(order[None, :] < order[:, None], lengths[0][None, :], 0), axis=1)

    def since_start(positions):
        begun = jnp.where(starts <= positions[..., None], starts, -1)
        return (positions - jnp.max(begun, axis=-1)).astype(F32)

    def spread(values):
        return jnp.broadcast_to(values[..., None], (*values.shape, LANES))

    stacked = jnp.concatenate([x[0, ROWS - 8 :] for x in (query_rows, key_rows, value_rows)], axis=0)
    halo = lax.ppermute(stacked, "ctx", [(i, i + 1) for i in range(count - 1)]).astype(F32)

    segs, steps = jnp.arange(SEGS, dtype=jnp.int32), jnp.arange(STEPS + HALO, dtype=jnp.int32)
    dist = spread(since_start(anchor + segs[None, :] * STEPS + steps[:, None]))
    seg_end = since_start(anchor + segs * STEPS + STEPS - 1)
    chain = []
    for k in range(3):
        chain.append((seg_end >= (STEPS << k)) & (segs >= (1 << k)))
    for k in range(3):
        ahead = jnp.minimum(segs + (1 << k) - 1, SEGS - 1)
        through = since_start(anchor + ahead * STEPS + STEPS - 1) >= (STEPS << k)
        chain.append(through & (segs + (1 << k) < SEGS))
    chain = spread(jnp.stack(chain).astype(F32))
    from_left = (since_start(anchor + segs * STEPS - 1) >= segs * STEPS) | (segs == 0)
    to_right = seg_end[SEGS - 1] >= (SEGS - 1 - segs) * STEPS
    reach = spread(jnp.stack([from_left, to_right]).astype(F32))
    seg_end = spread(seg_end)

    rate = decay_rate.T
    root = jnp.sqrt(rate)
    weight = residue.T * root
    decay = jnp.exp(-rate)
    taps = short_filter.reshape(3 * TAPS, channels)

    def passes(position, span):
        return (since_start(position) >= span).astype(F32) * jnp.exp(-rate * float(span))

    full = (ROWS, channels)
    states = (MODES * SEGS, channels)
    raw, feat, upstream, source, grad, gseg, sloc, rloc, end_state, begin_state = call(
        feature_kernel, "features",
        [((3, *full), F32), ((3, *full), F32), (full, F32), (full, F32), (full, F32),
         (states, F32), (states, F32), (states, F32), ((MODES, channels), F32), ((MODES, channels), F32)],
        [(4, ROWS, LANES), (HALO, STEPS, SEGS, LANES), (STEPS, SEGS, LANES), (STEPS, SEGS, LANES)],
        1 << 26,
        query_rows[0], key_rows[0], value_rows[0], cotangent[0], halo, taps, decay, dist, seg_end, chain,
    )

    pairs = [(i, i ^ 1) for i in range(count)]

    def onward(value, chips):
        moves = [(i, i + 2 * chips * (1 - 2 * (i % 2))) for i in range(count)]
        return lax.ppermute(value, "ctx", [(i, j) for i, j in moves if 0 <= j < count])

    lower = core == 0
    own = jnp.where(lower, end_state, begin_state)
    other = lax.ppermute(jnp.where(lower, begin_state, end_state), "ctx", pairs)
    partner_end = (here ^ 1) * ROWS + ROWS - 1
    own_pass = passes(anchor + ROWS - 1, ROWS)
    partner_pass = passes(partner_end, ROWS)
    chip_pass = passes(chip * 2 * ROWS + 2 * ROWS - 1, 2 * ROWS)
    far_pass = passes(jnp.where(lower, chip * 2 * ROWS - 1, (chip + 3) * 2 * ROWS - 1), 4 * ROWS)
    chip_state = other + partner_pass * own
    chip_state = chip_state + chip_pass * onward(chip_state, 1)
    near, far = onward(chip_state, 1), onward(chip_state, 3)
    arrived = near + far_pass * far
    handed = lax.ppermute(own + own_pass * arrived, "ctx", pairs)
    entering = jnp.where(lower, arrived, handed)
    returning = jnp.where(lower, handed, arrived)

    conv, back, swt, rwt, scoef, rcoef, local = call(
        local_kernel, "local_filter",
        [(full, F32), (full, F32), (states, F32), (states, F32), (states, F32), (states, F32),
         ((tiles, MODES + 8, LANES), F32)],
        [(STEPS - 1, STEPS, SEGS, LANES), (MODES, LANES)],
        1 << 26,
        source, grad, gseg, sloc, rloc, decay, rate, weight, skip_gain[None], dist, reach,
    )
    block_out, gfeat, edge, reduced = call(
        gradient_kernel, "filter_gradients",
        [(full, jnp.bfloat16), ((3, *full), F32), ((24, channels), F32), ((tiles, REDUCED, LANES), F32)],
        [(ROWS, LANES), (HALO, STEPS, SEGS, LANES), (STEPS, SEGS, LANES), (STEPS, SEGS, LANES)],
        1 << 26,
        raw, feat, upstream, conv, back, swt, rwt, scoef, rcoef, local,
        entering, returning, begin_state, decay, root, halo, dist, seg_end,
    )
    next_edge = lax.ppermute(edge, "ctx", [(i, i - 1) for i in range(1, count)])
    grad_query, grad_key, grad_value = call(
        input_kernel, "input_gradients",
        [(full, jnp.bfloat16)] * 3,
        [(3, ROWS, LANES), (HALO, STEPS + HALO, SEGS, LANES)],
        1 << 26,
        gfeat, next_edge, taps, dist,
    )

    place = lax.axis_index("dp")
    cuts = [("ctx", 1, core), ("dp", 2, place // 2), ("dp", 1, place % 2)]
    total = reduced

    def exchange(value, axis, flip):
        return lax.ppermute(value, axis, [(i, i ^ flip) for i in range(lax.axis_size(axis))])

    for axis, flip, bit in cuts:
        half = total.shape[0] // 2
        low, high = total[:half], total[half:]
        sent = exchange(jnp.where(bit == 0, high, low), axis, flip)
        total = jnp.where(bit == 0, low, high) + sent
    flip = 2
    while flip < count:
        total = total + exchange(total, "ctx", flip)
        flip *= 2
    for axis, flip, bit in reversed(cuts):
        other_half = exchange(total, axis, flip)
        total = jnp.where(
            bit == 0, jnp.concatenate([total, other_half]), jnp.concatenate([other_half, total])
        )
    total = total.transpose(1, 0, 2).reshape(REDUCED, channels)
    return (
        block_out[None],
        grad_query[None],
        grad_key[None],
        grad_value[None],
        total[MODES : MODES + 3 * TAPS].reshape(3, TAPS, channels),
        total[:MODES].T,
        total[MODES + 3 * TAPS],
    )


def solution(mesh):
    rows = P("dp", "ctx", "ch")
    return jax.shard_map(
        per_device,
        mesh=mesh,
        in_specs=(rows, rows, rows, rows, P("dp", None), P(None, None, "ch"), P("ch", None), P("ch", None), P("ch")),
        out_specs=(rows, rows, rows, rows, P(None, None, "ch"), P("ch", None), P("ch")),
        check_vma=False,
    )
```

```python
from functools import partial

import jax
import jax.numpy as jnp
from jax import lax
from jax.experimental import pallas as pl
from jax.experimental.pallas import tpu as pltpu
from jax.sharding import PartitionSpec as P

SEGS = 8
STEPS = 16
ROWS = SEGS * STEPS
TAPS = 7
HALO = TAPS - 1
MODES = 16
LANES = 128
REDUCED = 40
F32 = jnp.float32
BF16 = jnp.bfloat16
VMEM_BYTES = 12 << 20
CHUNKS = 4
RAW, FEAT, COT = 0, 3, 6
SOURCE, GRAD, GSEG, SLOC, RLOC = range(5)
CONV, BACK, SWT, RWT, SCOEF, RCOEF = range(6)


def slab(block, index):
    at = block * ROWS + index * SEGS
    return slice(at, at + SEGS)


def row(ref, index, lanes):
    return jnp.broadcast_to(ref[index : index + 1, lanes], (SEGS, LANES))


def starts_of(spot_ref):
    found, begun = [], jnp.int32(0)
    for j in range(2, spot_ref.shape[0]):
        found.append(begun)
        begun = begun + spot_ref[j]
    return found


def since_start(starts, positions):
    begun = jnp.zeros_like(positions)
    for start in starts:
        begun = jnp.where(positions >= start, start, begun)
    return positions - begun


def segments():
    return lax.broadcasted_iota(jnp.int32, (SEGS, LANES), 0)


def flag(condition):
    return jnp.where(condition, 1.0, 0.0)


def store_masks(starts, anchor, mask_ref, steps, gaps):
    for t in range(steps):
        dist = since_start(starts, anchor + segments() * STEPS + t)
        for gap in range(1, gaps + 1):
            mask_ref[gap - 1, t] = flag(dist >= gap)


def store_edge_masks(starts, anchor, open_mask, end_mask):
    at_end = since_start(starts, anchor + segments() * STEPS + STEPS - 1)
    for t in range(STEPS):
        dist = since_start(starts, anchor + segments() * STEPS + t)
        open_mask[t] = flag(dist >= t + 1)
        end_mask[t] = flag(at_end >= STEPS - 1 - t)


def each_tile(count, body):
    def step(index, carry):
        body(index, pl.ds(pl.multiple_of(index * LANES, LANES), LANES))
        return carry

    lax.fori_loop(0, count, step, 0)


def fetch_columns(ref, stage, lanes):
    stage[...] = ref[:, lanes].astype(F32)
    return [stage[pl.ds(t, SEGS, stride=STEPS), :] for t in range(STEPS)]


def rows_before(rows, halo_ref, branch, lanes):
    first = segments() == 0
    return {
        -back: jnp.where(first, row(halo_ref, branch * 8 + 8 - back, lanes), pltpu.roll(rows[STEPS - back], 1, 0))
        for back in range(1, HALO + 1)
    }


def feature_kernel(
    spot_ref, q_ref, k_ref, v_ref, cot_ref, taps_in, rate_in, residue_in, skip_in, halo_ref,
    save_ref, pre_ref, own_ref, sent_ref, pass_ref, taps_ref, rate_ref, residue_ref, skip_ref,
    stage, masks, open_mask, end_mask, chain, columns, arrived, loaded,
):
    starts, here = starts_of(spot_ref), spot_ref[0]
    anchor, core, chip = here * ROWS, here % 2, here // 2

    inputs = (q_ref, k_ref, v_ref, cot_ref)
    chunk = columns.shape[2] // CHUNKS

    def fetch(which, part):
        cols = pl.ds(pl.multiple_of(part * chunk, LANES), chunk)
        return pltpu.make_async_copy(inputs[which].at[:, cols], columns.at[which, :, cols], arrived.at[which, part])

    parameters = [
        pltpu.make_async_copy(source, target, loaded.at[which])
        for which, (source, target) in enumerate(
            ((taps_in, taps_ref), (rate_in, rate_ref), (residue_in, residue_ref), (skip_in, skip_ref))
        )
    ]
    for which in range(4):
        fetch(which, 0).start()
    for copy in parameters:
        copy.start()
    for part in range(1, CHUNKS):
        for which in range(4):
            fetch(which, part).start()
    store_masks(starts, anchor, masks, STEPS, HALO)
    store_edge_masks(starts, anchor, open_mask, end_mask)
    for k in range(3):
        span = STEPS << k
        at_end = since_start(starts, anchor + segments() * STEPS + STEPS - 1)
        chain[k] = flag((at_end >= span) & (segments() >= (1 << k)))
        ahead = jnp.minimum(segments() + (1 << k), SEGS)
        at_end = since_start(starts, anchor + ahead * STEPS - 1)
        chain[3 + k] = flag((at_end >= span) & (segments() + (1 << k) < SEGS))

    for copy in parameters:
        copy.wait()

    def passes(position, span):
        return flag(since_start(starts, position) >= span)

    far_end = jnp.where(core == 0, chip, chip + 3) * 2 * ROWS - 1
    own_pass = passes(anchor + ROWS - 1, ROWS)
    partner_pass = passes((here + 1 - 2 * core) * ROWS + ROWS - 1, ROWS)
    chip_pass = passes(chip * 2 * ROWS + 2 * ROWS - 1, 2 * ROWS)
    far_pass = passes(far_end, 4 * ROWS)
    lower = core == 0

    def tile_body(tile, lanes):
        segment = segments()
        first, last = segment == 0, segment == SEGS - 1

        @pl.when(tile % (chunk // LANES) == 0)
        def _():
            for which in range(4):
                fetch(which, tile // (chunk // LANES)).wait()

        for branch in range(3):
            rows = fetch_columns(columns.at[branch], stage.at[branch], lanes)
            before = rows_before(rows, halo_ref, branch, lanes)
            taps = [jnp.broadcast_to(taps_ref[branch, j : j + 1, lanes], (SEGS, LANES)) for j in range(TAPS)]
            for t in range(STEPS):
                save_ref[tile, slab(RAW + branch, t)] = rows[t]
                total = taps[0] * rows[t]
                for j in range(1, TAPS):
                    earlier = rows[t - j] if t >= j else before[t - j]
                    total = total + taps[j] * (earlier * masks[j - 1, t])
                save_ref[tile, slab(FEAT + branch, t)] = total
        upstream = fetch_columns(columns.at[3], stage.at[3], lanes)
        for t in range(STEPS):
            save_ref[tile, slab(COT, t)] = upstream[t]
            pre_ref[tile, slab(SOURCE, t)] = save_ref[tile, slab(FEAT + 1, t)] * save_ref[tile, slab(FEAT + 2, t)]
            pre_ref[tile, slab(GRAD, t)] = upstream[t] * save_ref[tile, slab(FEAT, t)]
        for low in range(0, MODES, 8):
            modes = range(low, low + 8)
            decay = [jnp.exp(-row(rate_ref, m, lanes)) for m in modes]
            ends = [pre_ref[tile, slab(SOURCE, 0)] * end_mask[0]] * 8
            for t in range(1, STEPS):
                value = pre_ref[tile, slab(SOURCE, t)] * end_mask[t]
                ends = [d * e + value for d, e in zip(decay, ends)]
            begins = [pre_ref[tile, slab(GRAD, STEPS - 1)] * open_mask[STEPS - 1]] * 8
            for t in range(STEPS - 2, -1, -1):
                value = pre_ref[tile, slab(GRAD, t)] * open_mask[t]
                begins = [d * b + value for d, b in zip(decay, begins)]
            for m, d, e, b in zip(modes, decay, ends, begins):
                pre_ref[tile, slab(GSEG, m)] = b
                for _ in range(4):
                    d = d * d
                for k in range(3):
                    e = e + (d * chain[k]) * pltpu.roll(e, 1 << k, 0)
                    b = b + (d * chain[3 + k]) * pltpu.roll(b, SEGS - (1 << k), 0)
                    d = d * d
                pre_ref[tile, slab(SLOC, m)] = jnp.where(first, 0.0, pltpu.roll(e, 1, 0))
                pre_ref[tile, slab(RLOC, m)] = jnp.where(last, 0.0, pltpu.roll(b, SEGS - 1, 0))
                own_ref[m : m + 1, lanes] = jnp.where(lower, e[SEGS - 1 :], b[:1])
                sent_ref[m : m + 1, lanes] = jnp.where(lower, b[:1], e[SEGS - 1 :])
        power = jnp.exp(rate_ref[:, lanes] * -float(ROWS))
        pass_ref[0, :, lanes] = own_pass * power
        pass_ref[1, :, lanes] = partner_pass * power
        power = power * power
        pass_ref[2, :, lanes] = chip_pass * power
        pass_ref[3, :, lanes] = far_pass * (power * power)

    each_tile(save_ref.shape[0], tile_body)


def local_kernel(
    spot_ref, pre_ref, rate_ref, residue_ref, skip_ref,
    post_ref, local_ref,
    masks, reach, stage, weight_stage,
):
    starts, anchor = starts_of(spot_ref), spot_ref[0] * ROWS

    store_masks(starts, anchor, masks, STEPS, STEPS - 1)
    before = since_start(starts, anchor + segments() * STEPS - 1)
    reach[0] = flag((before >= segments() * STEPS) | (segments() == 0))
    at_end = since_start(starts, anchor + segments() * 0 + ROWS - 1)
    reach[1] = flag(at_end >= (SEGS - 1 - segments()) * STEPS)

    def tile_body(tile, lanes):
        segment = segments().astype(F32)
        rates = rate_ref[:, lanes]
        decay = jnp.exp(-rates)
        power = residue_ref[:, lanes] * jnp.sqrt(rates)
        weight_stage[...] = power * decay
        kernel = []
        for gap in range(STEPS):
            kernel.append(jnp.sum(power, axis=0, keepdims=True))
            power = power * decay
        kernel[0] = kernel[0] + skip_ref[:, lanes]
        source = [pre_ref[tile, slab(SOURCE, t)] for t in range(STEPS)]
        grads = [pre_ref[tile, slab(GRAD, t)] for t in range(STEPS)]
        conv, back, paired = [None] * STEPS, [None] * STEPS, []
        for gap in range(STEPS):
            weight = jnp.broadcast_to(kernel[gap], (SEGS, LANES))
            pair = jnp.zeros((SEGS, LANES), F32)
            for t in range(gap, STEPS):
                value, grad = source[t - gap], grads[t]
                if gap:
                    value, grad = value * masks[gap - 1, t], grad * masks[gap - 1, t]
                conv[t] = weight * value if gap == 0 else conv[t] + weight * value
                back[t - gap] = weight * grad if gap == 0 else back[t - gap] + weight * grad
                pair = pair + grads[t] * value
            paired.append(jnp.sum(pair, axis=0, keepdims=True))
        for t in range(STEPS):
            post_ref[tile, slab(CONV, t)] = conv[t]
            post_ref[tile, slab(BACK, t)] = back[t]
        total = jnp.broadcast_to(paired[STEPS - 1], (MODES, LANES))
        for gap in range(STEPS - 2, -1, -1):
            total = total * decay + paired[gap]
        for m in range(MODES):
            arriving = pre_ref[tile, slab(SLOC, m)]
            stage[m : m + 1, :] = jnp.sum(arriving * pre_ref[tile, slab(GSEG, m)], axis=0, keepdims=True)
            scale = row(weight_stage, m, slice(None))
            rate = row(rate_ref, m, lanes) * (-float(STEPS))
            post_ref[tile, slab(SWT, m)] = scale * arriving
            post_ref[tile, slab(RWT, m)] = scale * pre_ref[tile, slab(RLOC, m)]
            post_ref[tile, slab(SCOEF, m)] = scale * reach[0] * jnp.exp(rate * segment)
            post_ref[tile, slab(RCOEF, m)] = scale * reach[1] * jnp.exp(rate * (SEGS - 1 - segment))
        local_ref[tile, 0:MODES] = total + stage[...] * decay
        local_ref[tile, MODES : MODES + 8] = jnp.broadcast_to(paired[0], (8, LANES))

    each_tile(pre_ref.shape[0], tile_body)


def tree_sum(values):
    while len(values) > 1:
        values = [a + b for a, b in zip(values[::2], values[1::2])]
    return values[0]


def tile_slot(tile, spot_ref):
    core, place = spot_ref[0] % 2, spot_ref[1]
    half = jnp.where(tile // 8 == core, 0, 1)
    slot = tile % 8
    high, low = slot // 4, (slot // 2) % 2
    high = jnp.where(high == place // 2, 0, 1)
    low = jnp.where(low == place % 2, 0, 1)
    return half, high * 4 + low * 2 + slot % 2


def gradient_kernel(
    spot_ref, save_ref, post_ref, local_ref, arrived_ref, handed_ref, own_ref, sent_ref, rate_ref, halo_ref,
    out_ref, gfeat_ref, edge_ref, kept_ref, away_ref,
    stage, masks, open_mask, end_mask, parts,
):
    starts, anchor = starts_of(spot_ref), spot_ref[0] * ROWS
    lower = spot_ref[0] % 2 == 0

    store_masks(starts, anchor, masks, STEPS, HALO)
    store_edge_masks(starts, anchor, open_mask, end_mask)

    def tile_body(tile, lanes):
        decay = [jnp.exp(-row(rate_ref, m, lanes)) for m in range(MODES)]
        arrived, handed = arrived_ref[:, lanes], handed_ref[:, lanes]
        entering = jnp.where(lower, arrived, handed)
        parts[0:MODES] = entering
        parts[MODES:] = jnp.where(lower, handed, arrived)
        state = [
            post_ref[tile, slab(SWT, m)] + post_ref[tile, slab(SCOEF, m)] * row(parts, m, slice(None))
            for m in range(MODES)
        ]
        for t in range(STEPS):
            filtered = post_ref[tile, slab(CONV, t)] + open_mask[t] * tree_sum(state)
            stage[pl.ds(t, SEGS, stride=STEPS), :] = save_ref[tile, slab(FEAT, t)] * filtered
            gfeat_ref[tile, slab(0, t)] = save_ref[tile, slab(COT, t)] * filtered
            if t < STEPS - 1:
                state = [d * s for d, s in zip(decay, state)]
        out_ref[:, lanes] = stage[...].astype(out_ref.dtype)
        state = [
            post_ref[tile, slab(RWT, m)] + post_ref[tile, slab(RCOEF, m)] * row(parts, MODES + m, slice(None))
            for m in range(MODES)
        ]
        for t in range(STEPS - 1, -1, -1):
            grad = post_ref[tile, slab(BACK, t)] + end_mask[t] * tree_sum(state)
            gfeat_ref[tile, slab(1, t)] = grad * save_ref[tile, slab(FEAT + 2, t)]
            gfeat_ref[tile, slab(2, t)] = grad * save_ref[tile, slab(FEAT + 1, t)]
            if t:
                state = [d * s for d, s in zip(decay, state)]
        rates = rate_ref[:, lanes]
        begin = jnp.where(lower, sent_ref[:, lanes], own_ref[:, lanes])
        sums = [jnp.sqrt(rates) * (local_ref[tile, 0:MODES] + entering * jnp.exp(-rates) * begin)]
        for branch in range(3):
            totals = [jnp.zeros((SEGS, LANES), F32)] * TAPS
            rows = [save_ref[tile, slab(RAW + branch, t)] for t in range(STEPS)]
            before = rows_before(rows, halo_ref, branch, lanes)
            for t in range(STEPS):
                grad = gfeat_ref[tile, slab(branch, t)]
                if t < HALO:
                    edge_ref[branch * 8 + t : branch * 8 + t + 1, lanes] = grad[:1]
                totals[0] = totals[0] + grad * rows[t]
                for j in range(1, TAPS):
                    earlier = rows[t - j] if t >= j else before[t - j]
                    totals[j] = totals[j] + (grad * masks[j - 1, t]) * earlier
            edge_ref[branch * 8 + HALO : branch * 8 + 8, lanes] = jnp.zeros((8 - HALO, LANES), F32)
            sums += [jnp.sum(total, axis=0, keepdims=True) for total in totals]
        sums.append(local_ref[tile, MODES : MODES + REDUCED - MODES - 3 * TAPS])
        half, slot = tile_slot(tile, spot_ref)
        for which, ref in enumerate((kept_ref, away_ref)):

            @pl.when(half == which)
            def _(ref=ref):
                at = 0
                for piece in sums:
                    ref[slot, at : at + piece.shape[0]] = piece
                    at += piece.shape[0]

    each_tile(save_ref.shape[0], tile_body)


def input_kernel(branch, spot_ref, gfeat_ref, edge_ref, taps_ref, out_ref, stage, masks):
    store_masks(starts_of(spot_ref), spot_ref[0] * ROWS, masks, STEPS + HALO, HALO)

    def tile_body(tile, lanes):
        last = segments() == SEGS - 1
        rows = [gfeat_ref[tile, slab(branch, t)] for t in range(STEPS)]
        for t in range(HALO):
            edge = row(edge_ref, branch * 8 + t, lanes)
            rows.append(jnp.where(last, edge, pltpu.roll(rows[t], SEGS - 1, 0)))
        taps = [jnp.broadcast_to(taps_ref[branch, j : j + 1, lanes], (SEGS, LANES)) for j in range(TAPS)]
        for t in range(STEPS):
            total = taps[0] * rows[t]
            for j in range(1, TAPS):
                total = total + taps[j] * (rows[t + j] * masks[j - 1, t + j])
            stage[pl.ds(t, SEGS, stride=STEPS), :] = total
        out_ref[:, lanes] = stage[...].astype(out_ref.dtype)

    each_tile(gfeat_ref.shape[0], tile_body)


def result_kernel(spot_ref, kept_ref, away_ref, short_ref, residue_ref, skip_ref):
    def tile_body(tile, lanes):
        half, slot = tile_slot(tile, spot_ref)
        block = jnp.where(half == 0, kept_ref[slot], away_ref[slot])
        for branch in range(3):
            at = MODES + branch * TAPS
            short_ref[branch, :, lanes] = block[at : at + TAPS]
        residue_ref[:, lanes] = block[:MODES]
        at = MODES + 3 * TAPS
        skip_ref[:, lanes] = block[at : at + 1]

    each_tile(kept_ref.shape[0] * 2, tile_body)


def combine_kernel(which, first_ref, pass_ref, second_ref, out_ref):
    out_ref[...] = first_ref[...] + pass_ref[which] * second_ref[...]


def arrive_kernel(near_ref, far_ref, own_ref, pass_ref, arrived_ref, handed_ref):
    arrived_ref[...] = near_ref[...] + pass_ref[3] * far_ref[...]
    handed_ref[...] = own_ref[...] + pass_ref[0] * arrived_ref[...]


SMEM, VMEM, HBM = (pl.BlockSpec(memory_space=space) for space in (pltpu.SMEM, pltpu.VMEM, pltpu.HBM))
MASKS = (HALO, STEPS, SEGS, LANES)
EDGE_MASKS = (STEPS, SEGS, LANES)
STAGE = (ROWS, LANES)


def call(body, name, ins, outs, scratch, *args):
    return pl.pallas_call(
        body,
        name=name,
        out_shape=[out if isinstance(out, jax.ShapeDtypeStruct) else pltpu.VMEM(out, F32) for out in outs],
        in_specs=ins,
        out_specs=[VMEM] * len(outs),
        scratch_shapes=[pltpu.VMEM(one, F32) if isinstance(one, tuple) else one for one in scratch],
        compiler_params=pltpu.CompilerParams(vmem_limit_bytes=VMEM_BYTES),
        cost_estimate=pl.CostEstimate(flops=1 << 26, bytes_accessed=8 << 20, transcendentals=0),
    )(*[x if spec is SMEM else pltpu.with_memory_space_constraint(x, spec.memory_space) for x, spec in zip(args, ins)])


def features(spot, query, key, value, upstream, taps, rate, residue, skip, halo):
    channels = query.shape[1]
    tiles, states = channels // LANES, (MODES, channels)
    return call(
        feature_kernel, "features",
        [SMEM] + [HBM] * 8 + [VMEM],
        [(tiles, 7 * ROWS, LANES), (tiles, 5 * ROWS, LANES), states, states, (4, *states),
         taps.shape, rate.shape, residue.shape, skip.shape],
        [(4, *STAGE), MASKS, EDGE_MASKS, EDGE_MASKS, (6, SEGS, LANES),
         pltpu.VMEM((4, ROWS, channels), BF16), pltpu.SemaphoreType.DMA((4, CHUNKS)), pltpu.SemaphoreType.DMA((4,))],
        spot, query, key, value, upstream, taps, rate, residue, skip, halo,
    )


def local_filter(spot, pre, rate, residue, skip):
    tiles = pre.shape[0]
    return call(
        local_kernel, "local_filter",
        [SMEM, VMEM, VMEM, VMEM, VMEM],
        [(tiles, 6 * ROWS, LANES), (tiles, MODES + 8, LANES)],
        [(STEPS - 1, STEPS, SEGS, LANES), (2, SEGS, LANES), (MODES, LANES), (MODES, LANES)],
        spot, pre, rate, residue, skip,
    )


def filter_gradients(spot, save, post, local, arrived, handed, own, sent, rate, halo):
    tiles, channels = save.shape[0], rate.shape[1]
    half = (tiles // 2, REDUCED, LANES)
    return call(
        gradient_kernel, "filter_gradients",
        [SMEM] + [VMEM] * 9,
        [jax.ShapeDtypeStruct((ROWS, channels), BF16), (tiles, 3 * ROWS, LANES), (24, channels), half, half],
        [STAGE, MASKS, EDGE_MASKS, EDGE_MASKS, (2 * MODES, LANES)],
        spot, save, post, local, arrived, handed, own, sent, rate, halo,
    )


def input_gradient(branch, spot, gfeat, edge, taps):
    [made] = call(
        partial(input_kernel, branch), "input_gradient",
        [SMEM, VMEM, VMEM, VMEM],
        [jax.ShapeDtypeStruct((ROWS, taps.shape[2]), BF16)],
        [STAGE, (HALO, STEPS + HALO, SEGS, LANES)],
        spot, gfeat, edge, taps,
    )
    return made


def results(spot, kept, away):
    channels = 2 * kept.shape[0] * LANES
    shapes = (3, TAPS, channels), (MODES, channels), (1, channels)
    return call(
        result_kernel, "parameter_gradients",
        [SMEM, VMEM, VMEM], [jax.ShapeDtypeStruct(shape, F32) for shape in shapes], [], spot, kept, away,
    )


def combine(which, first, through, second):
    [made] = call(
        partial(combine_kernel, which), "combine", [VMEM] * 3, [first.shape], [], first, through, second
    )
    return made


def per_device(query_rows, key_rows, value_rows, cotangent, lengths, short_filter, residue, decay_rate, skip_gain):
    count = lax.axis_size("ctx")
    place = jnp.stack([lax.axis_index("ctx"), lax.axis_index("dp")]).astype(jnp.int32)
    spot = jnp.concatenate([place, lengths[0]])

    stacked = jnp.concatenate([x[0, ROWS - 8 :] for x in (query_rows, key_rows, value_rows)], axis=0)
    halo = lax.ppermute(stacked, "ctx", [(i, i + 1) for i in range(count - 1)]).astype(F32)
    save, pre, own, sent, through, taps, rate, residue, skip = features(
        spot, query_rows[0], key_rows[0], value_rows[0], cotangent[0],
        short_filter, decay_rate.T, residue.T, skip_gain[None], halo,
    )

    pairs = [(i, i ^ 1) for i in range(count)]

    def onward(value, chips):
        moves = [(i, i + 2 * chips * (1 - 2 * (i % 2))) for i in range(count)]
        return lax.ppermute(value, "ctx", [(i, j) for i, j in moves if 0 <= j < count])

    chip_state = combine(1, lax.ppermute(sent, "ctx", pairs), through, own)
    chip_state = combine(2, chip_state, through, onward(chip_state, 1))
    chip_state, pre = lax.optimization_barrier((chip_state, pre))
    near, far = onward(chip_state, 1), onward(chip_state, 3)
    post, local = local_filter(spot, pre, rate, residue, skip)
    far, post = lax.optimization_barrier((far, post))
    arrived, handed = call(
        arrive_kernel, "arrive", [VMEM] * 4, [own.shape, own.shape], [], near, far, own, through
    )
    handed = lax.ppermute(handed, "ctx", pairs)

    block_out, gfeat, edge, kept, away = filter_gradients(
        spot, save, post, local, arrived, handed, own, sent, rate, halo
    )
    next_edge = lax.ppermute(edge, "ctx", [(i, i - 1) for i in range(1, count)])

    def exchange(value, axis, flip):
        return lax.ppermute(value, axis, [(i, i ^ flip) for i in range(lax.axis_size(axis))])

    grad_inputs = []

    def exchange_beside(value, axis, flip):
        value, beside = lax.optimization_barrier((value, next_edge))
        made = input_gradient(len(grad_inputs), spot, gfeat, beside, taps)
        sent, made = lax.optimization_barrier((exchange(value, axis, flip), made))
        grad_inputs.append(made)
        return sent

    received, next_edge = lax.optimization_barrier((exchange(away, "ctx", 1), next_edge))
    total = kept + received
    for flip in (2, 1):
        half = total.shape[0] // 2
        total = total[:half] + exchange(total[half:], "dp", flip)
    for flip in (2, 4, 8):
        total = total + exchange_beside(total, "ctx", flip)
    for flip in (1, 2):
        total = jnp.concatenate([total, exchange(total, "dp", flip)])
    grad_short, grad_residue, grad_skip = results(spot, total, exchange(total, "ctx", 1))
    return (block_out[None], *(g[None] for g in grad_inputs), grad_short, grad_residue.T, grad_skip[0])


def solution(mesh):
    rows = P("dp", "ctx", "ch")
    return jax.shard_map(
        per_device,
        mesh=mesh,
        in_specs=(rows, rows, rows, rows, P("dp", None), P(None, None, "ch"), P("ch", None), P("ch", None), P("ch")),
        out_specs=(rows, rows, rows, rows, P(None, None, "ch"), P("ch", None), P("ch")),
        check_vma=False,
    )
```

```python
from functools import partial

import jax
import jax.numpy as jnp
from jax import lax
from jax.experimental import pallas as pl
from jax.experimental.pallas import tpu as pltpu
from jax.sharding import PartitionSpec as P

SEGS = 8
STEPS = 16
ROWS = SEGS * STEPS
TAPS = 7
HALO = TAPS - 1
MODES = 16
LANES = 128
REDUCED = 40
F32 = jnp.float32
BF16 = jnp.bfloat16
VMEM_BYTES = 12 << 20
CHUNKS = 4
COT = 3
SOURCE, GRAD, GSEG, SLOC, RLOC = range(5)
CONV, BACK, SWT, RWT, SCOEF, RCOEF = range(6)
NEAR_TERMS, FAR_TERMS, CONV_ROWS, BACK_ROWS, FIRST_ROWS = 0, HALO * MODES, 2 * HALO * MODES, 2 * HALO * MODES + 8, 208


def slab(block, index):
    at = block * ROWS + index * SEGS
    return slice(at, at + SEGS)


def row(ref, index, lanes):
    return jnp.broadcast_to(ref[index : index + 1, lanes], (SEGS, LANES))


def starts_of(spot_ref):
    found, begun = [], jnp.int32(0)
    for j in range(2, spot_ref.shape[0]):
        found.append(begun)
        begun = begun + spot_ref[j]
    return found


def since_start(starts, positions):
    begun = jnp.zeros_like(positions)
    for start in starts:
        begun = jnp.where(positions >= start, start, begun)
    return positions - begun


def segments():
    return lax.broadcasted_iota(jnp.int32, (SEGS, LANES), 0)


def flag(condition):
    return jnp.where(condition, 1.0, 0.0)


def store_masks(starts, anchor, mask_ref, steps, gaps):
    for t in range(steps):
        dist = since_start(starts, anchor + segments() * STEPS + t)
        for gap in range(1, gaps + 1):
            mask_ref[gap - 1, t] = flag(dist >= gap)


def store_edge_masks(starts, anchor, open_mask, end_mask):
    at_end = since_start(starts, anchor + segments() * STEPS + STEPS - 1)
    for t in range(STEPS):
        dist = since_start(starts, anchor + segments() * STEPS + t)
        open_mask[t] = flag(dist >= t + 1)
        end_mask[t] = flag(at_end >= STEPS - 1 - t)


def each_tile(count, body):
    def step(index, carry):
        body(index, pl.ds(pl.multiple_of(index * LANES, LANES), LANES))
        return carry

    lax.fori_loop(0, count, step, 0)


def fetch_columns(ref, stage, lanes):
    stage[...] = ref[:, lanes].astype(F32)
    return [stage[pl.ds(t, SEGS, stride=STEPS), :] for t in range(STEPS)]


def rows_before(rows, halo_ref, branch, lanes):
    first = segments() == 0
    return {
        -back: jnp.where(first, row(halo_ref, branch * 8 + 8 - back, lanes), pltpu.roll(rows[STEPS - back], 1, 0))
        for back in range(1, HALO + 1)
    }


def stage_kernel(
    spot_ref, q_ref, k_ref, v_ref, cot_ref, taps_in, rate_in, residue_in, skip_in,
    raw_ref, masks, open_mask, end_mask, chain, taps_ref, rate_ref, residue_ref, skip_ref,
    stage, columns, arrived, loaded,
):
    inputs = (q_ref, k_ref, v_ref, cot_ref)
    chunk = columns.shape[2] // CHUNKS
    starts, anchor = starts_of(spot_ref), spot_ref[0] * ROWS

    def fetch(which, part):
        cols = pl.ds(pl.multiple_of(part * chunk, LANES), chunk)
        return pltpu.make_async_copy(inputs[which].at[:, cols], columns.at[which, :, cols], arrived.at[which, part])

    parameters = [
        pltpu.make_async_copy(source, target, loaded.at[which])
        for which, (source, target) in enumerate(
            ((taps_in, taps_ref), (rate_in, rate_ref), (residue_in, residue_ref), (skip_in, skip_ref))
        )
    ]
    for part in range(CHUNKS):
        for which in range(4):
            fetch(which, part).start()
    for copy in parameters:
        copy.start()
    store_masks(starts, anchor, masks, STEPS + HALO, HALO)
    store_edge_masks(starts, anchor, open_mask, end_mask)
    for k in range(3):
        span = STEPS << k
        at_end = since_start(starts, anchor + segments() * STEPS + STEPS - 1)
        chain[k] = flag((at_end >= span) & (segments() >= (1 << k)))
        ahead = jnp.minimum(segments() + (1 << k), SEGS)
        at_end = since_start(starts, anchor + ahead * STEPS - 1)
        chain[3 + k] = flag((at_end >= span) & (segments() + (1 << k) < SEGS))

    def tile_body(tile, lanes):
        @pl.when(tile % (chunk // LANES) == 0)
        def _():
            for which in range(4):
                fetch(which, tile // (chunk // LANES)).wait()

        for which in range(4):
            rows = fetch_columns(columns.at[which], stage.at[which], lanes)
            for t in range(STEPS):
                raw_ref[tile, slab(which, t)] = rows[t]

    each_tile(raw_ref.shape[0], tile_body)
    for copy in parameters:
        copy.wait()


def feature_kernel(
    spot_ref, raw_ref, masks, open_mask, end_mask, chain, taps_ref, rate_ref, halo_ref,
    feat_ref, pre_ref, own_ref, sent_ref, pass_ref,
):
    starts, here = starts_of(spot_ref), spot_ref[0]
    anchor, core, chip = here * ROWS, here % 2, here // 2

    def passes(position, span):
        return flag(since_start(starts, position) >= span)

    far_end = jnp.where(core == 0, chip, chip + 3) * 2 * ROWS - 1
    own_pass = passes(anchor + ROWS - 1, ROWS)
    partner_pass = passes((here + 1 - 2 * core) * ROWS + ROWS - 1, ROWS)
    chip_pass = passes(chip * 2 * ROWS + 2 * ROWS - 1, 2 * ROWS)
    far_pass = passes(far_end, 4 * ROWS)
    lower = core == 0

    def tile_body(tile, lanes):
        segment = segments()
        first, last = segment == 0, segment == SEGS - 1
        for branch in range(3):
            rows = [raw_ref[tile, slab(branch, t)] for t in range(STEPS)]
            before = rows_before(rows, halo_ref, branch, lanes)
            taps = [jnp.broadcast_to(taps_ref[branch, j : j + 1, lanes], (SEGS, LANES)) for j in range(TAPS)]
            for t in range(STEPS):
                total = taps[0] * rows[t]
                for j in range(1, TAPS):
                    earlier = rows[t - j] if t >= j else before[t - j]
                    total = total + taps[j] * (earlier * masks[j - 1, t])
                feat_ref[tile, slab(branch, t)] = total
        for t in range(STEPS):
            pre_ref[tile, slab(SOURCE, t)] = feat_ref[tile, slab(1, t)] * feat_ref[tile, slab(2, t)]
            pre_ref[tile, slab(GRAD, t)] = raw_ref[tile, slab(COT, t)] * feat_ref[tile, slab(0, t)]
        for low in range(0, MODES, 8):
            modes = range(low, low + 8)
            decay = [jnp.exp(-row(rate_ref, m, lanes)) for m in modes]
            ends = [pre_ref[tile, slab(SOURCE, 0)] * end_mask[0]] * 8
            for t in range(1, STEPS):
                value = pre_ref[tile, slab(SOURCE, t)] * end_mask[t]
                ends = [d * e + value for d, e in zip(decay, ends)]
            begins = [pre_ref[tile, slab(GRAD, STEPS - 1)] * open_mask[STEPS - 1]] * 8
            for t in range(STEPS - 2, -1, -1):
                value = pre_ref[tile, slab(GRAD, t)] * open_mask[t]
                begins = [d * b + value for d, b in zip(decay, begins)]
            for m, d, e, b in zip(modes, decay, ends, begins):
                pre_ref[tile, slab(GSEG, m)] = b
                for _ in range(4):
                    d = d * d
                for k in range(3):
                    e = e + (d * chain[k]) * pltpu.roll(e, 1 << k, 0)
                    b = b + (d * chain[3 + k]) * pltpu.roll(b, SEGS - (1 << k), 0)
                    d = d * d
                pre_ref[tile, slab(SLOC, m)] = jnp.where(first, 0.0, pltpu.roll(e, 1, 0))
                pre_ref[tile, slab(RLOC, m)] = jnp.where(last, 0.0, pltpu.roll(b, SEGS - 1, 0))
                own_ref[m : m + 1, lanes] = jnp.where(lower, e[SEGS - 1 :], b[:1])
                sent_ref[m : m + 1, lanes] = jnp.where(lower, b[:1], e[SEGS - 1 :])
        power = jnp.exp(rate_ref[:, lanes] * -float(ROWS))
        pass_ref[0, :, lanes] = own_pass * power
        pass_ref[1, :, lanes] = partner_pass * power
        power = power * power
        pass_ref[2, :, lanes] = chip_pass * power
        pass_ref[3, :, lanes] = far_pass * (power * power)

    each_tile(raw_ref.shape[0], tile_body)


def local_kernel(
    spot_ref, pre_ref, rate_ref, residue_ref, skip_ref, open_mask, end_mask,
    post_ref, local_ref, first_ref,
    masks, reach, stage, weight_stage,
):
    starts, anchor = starts_of(spot_ref), spot_ref[0] * ROWS

    store_masks(starts, anchor, masks, STEPS, STEPS - 1)
    before = since_start(starts, anchor + segments() * STEPS - 1)
    reach[0] = flag((before >= segments() * STEPS) | (segments() == 0))
    at_end = since_start(starts, anchor + segments() * 0 + ROWS - 1)
    reach[1] = flag(at_end >= (SEGS - 1 - segments()) * STEPS)

    def tile_body(tile, lanes):
        segment = segments().astype(F32)
        rates = rate_ref[:, lanes]
        decay = jnp.exp(-rates)
        power = residue_ref[:, lanes] * jnp.sqrt(rates)
        weight_stage[...] = power * decay
        kernel = []
        for gap in range(STEPS):
            kernel.append(jnp.sum(power, axis=0, keepdims=True))
            power = power * decay
        kernel[0] = kernel[0] + skip_ref[:, lanes]
        source = [pre_ref[tile, slab(SOURCE, t)] for t in range(STEPS)]
        grads = [pre_ref[tile, slab(GRAD, t)] for t in range(STEPS)]
        conv, back, paired = [None] * STEPS, [None] * STEPS, []
        for gap in range(STEPS):
            weight = jnp.broadcast_to(kernel[gap], (SEGS, LANES))
            pair = jnp.zeros((SEGS, LANES), F32)
            for t in range(gap, STEPS):
                value, grad = source[t - gap], grads[t]
                if gap:
                    value, grad = value * masks[gap - 1, t], grad * masks[gap - 1, t]
                conv[t] = weight * value if gap == 0 else conv[t] + weight * value
                back[t - gap] = weight * grad if gap == 0 else back[t - gap] + weight * grad
                pair = pair + grads[t] * value
            paired.append(jnp.sum(pair, axis=0, keepdims=True))
        for t in range(STEPS):
            post_ref[tile, slab(CONV, t)] = conv[t]
            post_ref[tile, slab(BACK, t)] = back[t]
        scaled = [weight_stage[...]]
        for t in range(1, STEPS):
            scaled.append(scaled[-1] * decay)
        later = pre_ref[tile, pl.ds(RLOC * ROWS, MODES, stride=SEGS), :]
        beyond = reach[1, :1] * jnp.exp(rates * -float(ROWS - STEPS))
        for t in range(HALO):
            far_term = end_mask[t, :1] * scaled[STEPS - 1 - t]
            first_ref[tile, NEAR_TERMS + t * MODES : NEAR_TERMS + (t + 1) * MODES] = open_mask[t, :1] * scaled[t]
            first_ref[tile, FAR_TERMS + t * MODES : FAR_TERMS + (t + 1) * MODES] = far_term * beyond
            back_row = back[t][:1] + jnp.sum(far_term * later, axis=0, keepdims=True)
            first_ref[tile, CONV_ROWS + t : CONV_ROWS + t + 1] = conv[t][:1]
            first_ref[tile, BACK_ROWS + t : BACK_ROWS + t + 1] = back_row
        total = jnp.broadcast_to(paired[STEPS - 1], (MODES, LANES))
        for gap in range(STEPS - 2, -1, -1):
            total = total * decay + paired[gap]
        for m in range(MODES):
            arriving = pre_ref[tile, slab(SLOC, m)]
            stage[m : m + 1, :] = jnp.sum(arriving * pre_ref[tile, slab(GSEG, m)], axis=0, keepdims=True)
            scale = row(weight_stage, m, slice(None))
            rate = row(rate_ref, m, lanes) * (-float(STEPS))
            post_ref[tile, slab(SWT, m)] = scale * arriving
            post_ref[tile, slab(RWT, m)] = scale * pre_ref[tile, slab(RLOC, m)]
            post_ref[tile, slab(SCOEF, m)] = scale * reach[0] * jnp.exp(rate * segment)
            post_ref[tile, slab(RCOEF, m)] = scale * reach[1] * jnp.exp(rate * (SEGS - 1 - segment))
        local_ref[tile, 0:MODES] = total + stage[...] * decay
        local_ref[tile, MODES : MODES + 8] = jnp.broadcast_to(paired[0], (8, LANES))

    each_tile(pre_ref.shape[0], tile_body)


def tree_sum(values):
    while len(values) > 1:
        values = [a + b for a, b in zip(values[::2], values[1::2])]
    return values[0]


def tile_slot(tile, spot_ref):
    core, place = spot_ref[0] % 2, spot_ref[1]
    half = jnp.where(tile // 8 == core, 0, 1)
    slot = tile % 8
    high, low = slot // 4, (slot // 2) % 2
    high = jnp.where(high == place // 2, 0, 1)
    low = jnp.where(low == place % 2, 0, 1)
    return half, high * 4 + low * 2 + slot % 2


def edge_kernel(
    spot_ref, raw_ref, feat_ref, first_ref, arrived_ref, handed_ref, enter_ref, return_ref, edge_ref
):
    lower = spot_ref[0] % 2 == 0

    def tile_body(tile, lanes):
        arrived, handed = arrived_ref[:, lanes], handed_ref[:, lanes]
        entering, returning = jnp.where(lower, arrived, handed), jnp.where(lower, handed, arrived)
        enter_ref[:, lanes] = entering
        return_ref[:, lanes] = returning
        for t in range(HALO):
            near = first_ref[tile, NEAR_TERMS + t * MODES : NEAR_TERMS + (t + 1) * MODES]
            far = first_ref[tile, FAR_TERMS + t * MODES : FAR_TERMS + (t + 1) * MODES]
            filtered = first_ref[tile, CONV_ROWS + t : CONV_ROWS + t + 1]
            filtered = filtered + jnp.sum(near * entering, axis=0, keepdims=True)
            grad = first_ref[tile, BACK_ROWS + t : BACK_ROWS + t + 1]
            grad = grad + jnp.sum(far * returning, axis=0, keepdims=True)
            edge_ref[t : t + 1, lanes] = raw_ref[tile, slab(COT, t)][:1] * filtered
            edge_ref[8 + t : 9 + t, lanes] = grad * feat_ref[tile, slab(2, t)][:1]
            edge_ref[16 + t : 17 + t, lanes] = grad * feat_ref[tile, slab(1, t)][:1]
        for branch in range(3):
            edge_ref[branch * 8 + HALO : branch * 8 + 8, lanes] = jnp.zeros((8 - HALO, LANES), F32)

    each_tile(raw_ref.shape[0], tile_body)


def gradient_kernel(
    spot_ref, raw_ref, feat_ref, post_ref, local_ref, enter_ref, return_ref, own_ref, sent_ref, rate_ref, halo_ref,
    masks, open_mask, end_mask,
    out_ref, gfeat_ref, kept_ref, away_ref,
    stage,
):
    lower = spot_ref[0] % 2 == 0

    def tile_body(tile, lanes):
        decay = [jnp.exp(-row(rate_ref, m, lanes)) for m in range(MODES)]
        state = [
            post_ref[tile, slab(SWT, m)] + post_ref[tile, slab(SCOEF, m)] * row(enter_ref, m, lanes)
            for m in range(MODES)
        ]
        for t in range(STEPS):
            filtered = post_ref[tile, slab(CONV, t)] + open_mask[t] * tree_sum(state)
            stage[pl.ds(t, SEGS, stride=STEPS), :] = feat_ref[tile, slab(0, t)] * filtered
            gfeat_ref[tile, slab(0, t)] = raw_ref[tile, slab(COT, t)] * filtered
            if t < STEPS - 1:
                state = [d * s for d, s in zip(decay, state)]
        out_ref[:, lanes] = stage[...].astype(out_ref.dtype)
        state = [
            post_ref[tile, slab(RWT, m)] + post_ref[tile, slab(RCOEF, m)] * row(return_ref, m, lanes)
            for m in range(MODES)
        ]
        for t in range(STEPS - 1, -1, -1):
            grad = post_ref[tile, slab(BACK, t)] + end_mask[t] * tree_sum(state)
            gfeat_ref[tile, slab(1, t)] = grad * feat_ref[tile, slab(2, t)]
            gfeat_ref[tile, slab(2, t)] = grad * feat_ref[tile, slab(1, t)]
            if t:
                state = [d * s for d, s in zip(decay, state)]
        rates = rate_ref[:, lanes]
        begin = jnp.where(lower, sent_ref[:, lanes], own_ref[:, lanes])
        sums = [jnp.sqrt(rates) * (local_ref[tile, 0:MODES] + enter_ref[:, lanes] * jnp.exp(-rates) * begin)]
        for branch in range(3):
            totals = [jnp.zeros((SEGS, LANES), F32)] * TAPS
            rows = [raw_ref[tile, slab(branch, t)] for t in range(STEPS)]
            before = rows_before(rows, halo_ref, branch, lanes)
            for t in range(STEPS):
                grad = gfeat_ref[tile, slab(branch, t)]
                totals[0] = totals[0] + grad * rows[t]
                for j in range(1, TAPS):
                    earlier = rows[t - j] if t >= j else before[t - j]
                    totals[j] = totals[j] + (grad * masks[j - 1, t]) * earlier
            sums += [jnp.sum(total, axis=0, keepdims=True) for total in totals]
        sums.append(local_ref[tile, MODES : MODES + REDUCED - MODES - 3 * TAPS])
        half, slot = tile_slot(tile, spot_ref)
        for which, ref in enumerate((kept_ref, away_ref)):

            @pl.when(half == which)
            def _(ref=ref):
                at = 0
                for piece in sums:
                    ref[slot, at : at + piece.shape[0]] = piece
                    at += piece.shape[0]

    each_tile(raw_ref.shape[0], tile_body)


def input_kernel(branch, gfeat_ref, edge_ref, taps_ref, masks, out_ref, stage):

    def tile_body(tile, lanes):
        last = segments() == SEGS - 1
        rows = [gfeat_ref[tile, slab(branch, t)] for t in range(STEPS)]
        for t in range(HALO):
            edge = row(edge_ref, branch * 8 + t, lanes)
            rows.append(jnp.where(last, edge, pltpu.roll(rows[t], SEGS - 1, 0)))
        taps = [jnp.broadcast_to(taps_ref[branch, j : j + 1, lanes], (SEGS, LANES)) for j in range(TAPS)]
        for t in range(STEPS):
            total = taps[0] * rows[t]
            for j in range(1, TAPS):
                total = total + taps[j] * (rows[t + j] * masks[j - 1, t + j])
            stage[pl.ds(t, SEGS, stride=STEPS), :] = total
        out_ref[:, lanes] = stage[...].astype(out_ref.dtype)

    each_tile(gfeat_ref.shape[0], tile_body)


def result_kernel(spot_ref, kept_ref, away_ref, short_ref, residue_ref, skip_ref):
    def tile_body(tile, lanes):
        half, slot = tile_slot(tile, spot_ref)
        block = jnp.where(half == 0, kept_ref[slot], away_ref[slot])
        for branch in range(3):
            at = MODES + branch * TAPS
            short_ref[branch, :, lanes] = block[at : at + TAPS]
        residue_ref[:, lanes] = block[:MODES]
        at = MODES + 3 * TAPS
        skip_ref[:, lanes] = block[at : at + 1]

    each_tile(kept_ref.shape[0] * 2, tile_body)


def combine_kernel(which, first_ref, pass_ref, second_ref, out_ref):
    out_ref[...] = first_ref[...] + pass_ref[which] * second_ref[...]


def arrive_kernel(near_ref, far_ref, own_ref, pass_ref, arrived_ref, handed_ref):
    arrived_ref[...] = near_ref[...] + pass_ref[3] * far_ref[...]
    handed_ref[...] = own_ref[...] + pass_ref[0] * arrived_ref[...]


SMEM, VMEM, HBM = (pl.BlockSpec(memory_space=space) for space in (pltpu.SMEM, pltpu.VMEM, pltpu.HBM))
MASKS = (HALO, STEPS + HALO, SEGS, LANES)
EDGE_MASKS = (STEPS, SEGS, LANES)
STAGE = (ROWS, LANES)


def call(body, name, ins, outs, scratch, *args):
    return pl.pallas_call(
        body,
        name=name,
        out_shape=[out if isinstance(out, jax.ShapeDtypeStruct) else pltpu.VMEM(out, F32) for out in outs],
        in_specs=ins,
        out_specs=[VMEM] * len(outs),
        scratch_shapes=[pltpu.VMEM(one, F32) if isinstance(one, tuple) else one for one in scratch],
        compiler_params=pltpu.CompilerParams(vmem_limit_bytes=VMEM_BYTES),
        cost_estimate=pl.CostEstimate(flops=1 << 26, bytes_accessed=8 << 20, transcendentals=0),
    )(*[x if spec is SMEM else pltpu.with_memory_space_constraint(x, spec.memory_space) for x, spec in zip(args, ins)])


def staged(spot, query, key, value, upstream, taps, rate, residue, skip):
    channels = query.shape[1]
    return call(
        stage_kernel, "stage",
        [SMEM] + [HBM] * 8,
        [(channels // LANES, 4 * ROWS, LANES), MASKS, EDGE_MASKS, EDGE_MASKS, (6, SEGS, LANES),
         taps.shape, rate.shape, residue.shape, skip.shape],
        [(4, *STAGE), pltpu.VMEM((4, ROWS, channels), BF16), pltpu.SemaphoreType.DMA((4, CHUNKS)),
         pltpu.SemaphoreType.DMA((4,))],
        spot, query, key, value, upstream, taps, rate, residue, skip,
    )


def features(spot, raw, masks, open_mask, end_mask, chain, taps, rate, halo):
    tiles, states = raw.shape[0], rate.shape
    return call(
        feature_kernel, "features",
        [SMEM] + [VMEM] * 8,
        [(tiles, 3 * ROWS, LANES), (tiles, 5 * ROWS, LANES), states, states, (4, *states)],
        [],
        spot, raw, masks, open_mask, end_mask, chain, taps, rate, halo,
    )


def local_filter(spot, pre, rate, residue, skip, open_mask, end_mask):
    tiles = pre.shape[0]
    return call(
        local_kernel, "local_filter",
        [SMEM] + [VMEM] * 6,
        [(tiles, 6 * ROWS, LANES), (tiles, MODES + 8, LANES), (tiles, FIRST_ROWS, LANES)],
        [(STEPS - 1, STEPS, SEGS, LANES), (2, SEGS, LANES), (MODES, LANES), (MODES, LANES)],
        spot, pre, rate, residue, skip, open_mask, end_mask,
    )


def edge_gradients(spot, raw, feat, first, arrived, handed):
    states = arrived.shape
    return call(
        edge_kernel, "edge_gradients", [SMEM] + [VMEM] * 5, [states, states, (24, states[1])], [],
        spot, raw, feat, first, arrived, handed,
    )


def filter_gradients(spot, raw, *others):
    tiles = raw.shape[0]
    half = (tiles // 2, REDUCED, LANES)
    return call(
        gradient_kernel, "filter_gradients",
        [SMEM] + [VMEM] * (1 + len(others)),
        [jax.ShapeDtypeStruct((ROWS, tiles * LANES), BF16), (tiles, 3 * ROWS, LANES), half, half],
        [STAGE],
        spot, raw, *others,
    )


def input_gradient(branch, gfeat, edge, taps, masks):
    [made] = call(
        partial(input_kernel, branch), "input_gradient",
        [VMEM] * 4,
        [jax.ShapeDtypeStruct((ROWS, taps.shape[2]), BF16)],
        [STAGE],
        gfeat, edge, taps, masks,
    )
    return made


def results(spot, kept, away):
    channels = 2 * kept.shape[0] * LANES
    shapes = (3, TAPS, channels), (MODES, channels), (1, channels)
    return call(
        result_kernel, "parameter_gradients",
        [SMEM, VMEM, VMEM], [jax.ShapeDtypeStruct(shape, F32) for shape in shapes], [], spot, kept, away,
    )


def combine(which, first, through, second):
    [made] = call(
        partial(combine_kernel, which), "combine", [VMEM] * 3, [first.shape], [], first, through, second
    )
    return made


def per_device(query_rows, key_rows, value_rows, cotangent, lengths, short_filter, residue, decay_rate, skip_gain):
    count = lax.axis_size("ctx")
    place = jnp.stack([lax.axis_index("ctx"), lax.axis_index("dp")]).astype(jnp.int32)
    spot = jnp.concatenate([place, lengths[0]])

    stacked = jnp.concatenate([x[0, ROWS - 8 :] for x in (query_rows, key_rows, value_rows)], axis=0)
    halo = lax.ppermute(stacked, "ctx", [(i, i + 1) for i in range(count - 1)]).astype(F32)
    raw, masks, open_mask, end_mask, chain, taps, rate, residue, skip = staged(
        spot, query_rows[0], key_rows[0], value_rows[0], cotangent[0],
        short_filter, decay_rate.T, residue.T, skip_gain[None],
    )
    feat, pre, own, sent, through = features(spot, raw, masks, open_mask, end_mask, chain, taps, rate, halo)

    pairs = [(i, i ^ 1) for i in range(count)]

    def onward(value, chips):
        moves = [(i, i + 2 * chips * (1 - 2 * (i % 2))) for i in range(count)]
        return lax.ppermute(value, "ctx", [(i, j) for i, j in moves if 0 <= j < count])

    chip_state = combine(1, lax.ppermute(sent, "ctx", pairs), through, own)
    chip_state = combine(2, chip_state, through, onward(chip_state, 1))
    chip_state, pre = lax.optimization_barrier((chip_state, pre))
    near, far = onward(chip_state, 1), onward(chip_state, 3)
    post, local, first = local_filter(spot, pre, rate, residue, skip, open_mask, end_mask)
    far, post = lax.optimization_barrier((far, post))
    arrived, handed = call(
        arrive_kernel, "arrive", [VMEM] * 4, [own.shape, own.shape], [], near, far, own, through
    )
    handed = lax.ppermute(handed, "ctx", pairs)

    entering, returning, edge = edge_gradients(spot, raw, feat, first, arrived, handed)
    next_edge = lax.ppermute(edge, "ctx", [(i, i - 1) for i in range(1, count)])
    block_out, gfeat, kept, away = filter_gradients(
        spot, raw, feat, post, local, entering, returning, own, sent, rate, halo, masks, open_mask, end_mask
    )
    away, next_edge = lax.optimization_barrier((away, next_edge))

    def exchange(value, axis, flip):
        return lax.ppermute(value, axis, [(i, i ^ flip) for i in range(lax.axis_size(axis))])

    grad_inputs = []

    def exchange_beside(value, axis, flip):
        value, beside = lax.optimization_barrier((value, next_edge))
        made = input_gradient(len(grad_inputs), gfeat, beside, taps, masks)
        sent, made = lax.optimization_barrier((exchange(value, axis, flip), made))
        grad_inputs.append(made)
        return sent

    total = kept + exchange(away, "ctx", 1)
    for flip in (2, 1):
        half = total.shape[0] // 2
        total = total[:half] + exchange(total[half:], "dp", flip)
    for flip in (2, 4, 8):
        total = total + exchange_beside(total, "ctx", flip)
    for flip in (1, 2):
        total = jnp.concatenate([total, exchange(total, "dp", flip)])
    grad_short, grad_residue, grad_skip = results(spot, total, exchange(total, "ctx", 1))
    return (block_out[None], *(g[None] for g in grad_inputs), grad_short, grad_residue.T, grad_skip[0])


def solution(mesh):
    rows = P("dp", "ctx", "ch")
    return jax.shard_map(
        per_device,
        mesh=mesh,
        in_specs=(rows, rows, rows, rows, P("dp", None), P(None, None, "ch"), P("ch", None), P("ch", None), P("ch")),
        out_specs=(rows, rows, rows, rows, P(None, None, "ch"), P("ch", None), P("ch")),
        check_vma=False,
    )
```

```python
from functools import partial

import jax
import jax.numpy as jnp
from jax import lax
from jax.experimental import pallas as pl
from jax.experimental.pallas import tpu as pltpu
from jax.sharding import PartitionSpec as P

SEGS = 8
STEPS = 16
ROWS = SEGS * STEPS
TAPS = 7
HALO = TAPS - 1
MODES = 16
LANES = 128
REDUCED = 40
F32 = jnp.float32
BF16 = jnp.bfloat16
VMEM_BYTES = 12 << 20
CHUNKS = 4
COT = 3
SOURCE, GRAD, GSEG, SLOC, RLOC = range(5)
CONV, BACK, SWT, RWT, SCOEF, RCOEF = range(6)
NEAR_TERMS, FAR_TERMS, CONV_ROWS, BACK_ROWS, FIRST_ROWS = 0, HALO * MODES, 2 * HALO * MODES, 2 * HALO * MODES + 8, 208


def slab(block, index):
    at = block * ROWS + index * SEGS
    return slice(at, at + SEGS)


def row(ref, index, lanes):
    return jnp.broadcast_to(ref[index : index + 1, lanes], (SEGS, LANES))


def starts_of(spot_ref):
    return sums_before([spot_ref[j] for j in range(2, spot_ref.shape[0])])


def sums_before(lengths):
    found = [jnp.int32(0)]
    for length in lengths[:-1]:
        found.append(found[-1] + length)
    return found


def since_start(starts, positions):
    begun = jnp.zeros_like(positions)
    for start in starts:
        begun = jnp.where(positions >= start, start, begun)
    return positions - begun


def segments():
    return lax.broadcasted_iota(jnp.int32, (SEGS, LANES), 0)


def flag(condition):
    return jnp.where(condition, 1.0, 0.0)


def store_masks(starts, anchor, mask_ref, steps, gaps):
    for t in range(steps):
        dist = since_start(starts, anchor + segments() * STEPS + t)
        for gap in range(1, gaps + 1):
            mask_ref[gap - 1, t] = flag(dist >= gap)


def store_edge_masks(starts, anchor, open_mask, end_mask):
    at_end = since_start(starts, anchor + segments() * STEPS + STEPS - 1)
    for t in range(STEPS):
        dist = since_start(starts, anchor + segments() * STEPS + t)
        open_mask[t] = flag(dist >= t + 1)
        end_mask[t] = flag(at_end >= STEPS - 1 - t)


def each_tile(count, body):
    def step(index, carry):
        body(index, pl.ds(pl.multiple_of(index * LANES, LANES), LANES))
        return carry

    lax.fori_loop(0, count, step, 0)


def fetch_columns(ref, stage, lanes):
    stage[...] = ref[:, lanes].astype(F32)
    return [stage[pl.ds(t, SEGS, stride=STEPS), :] for t in range(STEPS)]


def rows_before(rows, halo_ref, branch, lanes):
    first = segments() == 0
    return {
        -back: jnp.where(first, row(halo_ref, branch * 8 + 8 - back, lanes), pltpu.roll(rows[STEPS - back], 1, 0))
        for back in range(1, HALO + 1)
    }


def tail_kernel(q_ref, k_ref, v_ref, out_ref, rows, arrived):
    copies = [
        pltpu.make_async_copy(ref.at[ROWS - 16 :], rows.at[which], arrived.at[which])
        for which, ref in enumerate((q_ref, k_ref, v_ref))
    ]
    for copy in copies:
        copy.start()
    for copy in copies:
        copy.wait()

    def tile_body(tile, lanes):
        q, k, v = (rows[which, :, lanes].astype(F32)[8:] for which in range(3))
        out_ref[0:16, lanes] = jnp.concatenate([q, k], axis=0).astype(BF16)
        out_ref[16:32, lanes] = jnp.concatenate([v, jnp.zeros_like(v)], axis=0).astype(BF16)

    each_tile(out_ref.shape[1] // LANES, tile_body)


def stage_kernel(
    place_ref, lengths_in, q_ref, k_ref, v_ref, cot_ref, taps_in, rate_in, residue_in, skip_in,
    raw_ref, masks, open_mask, end_mask, chain, taps_ref, rate_ref, residue_ref, skip_ref, decay_ref,
    stage, columns, arrived, loaded, lengths_ref, known,
):
    inputs = (q_ref, k_ref, v_ref, cot_ref)
    chunk = columns.shape[2] // CHUNKS
    anchor = place_ref[0] * ROWS
    lengths = pltpu.make_async_copy(lengths_in, lengths_ref, known)
    lengths.start()

    def fetch(which, part):
        cols = pl.ds(pl.multiple_of(part * chunk, LANES), chunk)
        return pltpu.make_async_copy(inputs[which].at[:, cols], columns.at[which, :, cols], arrived.at[which, part])

    parameters = [
        pltpu.make_async_copy(source, target, loaded.at[which])
        for which, (source, target) in enumerate(
            ((taps_in, taps_ref), (rate_in, rate_ref), (residue_in, residue_ref), (skip_in, skip_ref))
        )
    ]
    for part in range(CHUNKS):
        for which in range(4):
            fetch(which, part).start()
    for copy in parameters:
        copy.start()
    lengths.wait()
    starts = sums_before([lengths_ref[0, j] for j in range(lengths_ref.shape[1])])
    store_masks(starts, anchor, masks, STEPS + HALO, HALO)
    store_edge_masks(starts, anchor, open_mask, end_mask)
    for k in range(3):
        span = STEPS << k
        at_end = since_start(starts, anchor + segments() * STEPS + STEPS - 1)
        chain[k] = flag((at_end >= span) & (segments() >= (1 << k)))
        ahead = jnp.minimum(segments() + (1 << k), SEGS)
        at_end = since_start(starts, anchor + ahead * STEPS - 1)
        chain[3 + k] = flag((at_end >= span) & (segments() + (1 << k) < SEGS))

    def tile_body(tile, lanes):
        @pl.when(tile % (chunk // LANES) == 0)
        def _():
            for which in range(4):
                fetch(which, tile // (chunk // LANES)).wait()

        for which in range(4):
            rows = fetch_columns(columns.at[which], stage.at[which], lanes)
            for t in range(STEPS):
                raw_ref[tile, slab(which, t)] = rows[t]

    each_tile(raw_ref.shape[0], tile_body)
    for copy in parameters:
        copy.wait()

    def decay_body(tile, lanes):
        decay_ref[:, lanes] = jnp.exp(-rate_ref[:, lanes])

    each_tile(raw_ref.shape[0], decay_body)


def feature_kernel(
    spot_ref, raw_ref, masks, open_mask, end_mask, chain, taps_ref, rate_ref, decay_ref, halo_ref,
    feat_ref, pre_ref, own_ref, sent_ref, pass_ref,
):
    starts, here = starts_of(spot_ref), spot_ref[0]
    anchor, core, chip = here * ROWS, here % 2, here // 2

    def passes(position, span):
        return flag(since_start(starts, position) >= span)

    far_end = jnp.where(core == 0, chip, chip + 3) * 2 * ROWS - 1
    own_pass = passes(anchor + ROWS - 1, ROWS)
    partner_pass = passes((here + 1 - 2 * core) * ROWS + ROWS - 1, ROWS)
    chip_pass = passes(chip * 2 * ROWS + 2 * ROWS - 1, 2 * ROWS)
    far_pass = passes(far_end, 4 * ROWS)
    lower = core == 0

    def tile_body(tile, lanes):
        segment = segments()
        first, last = segment == 0, segment == SEGS - 1
        for branch in range(3):
            rows = [raw_ref[tile, slab(branch, t)] for t in range(STEPS)]
            before = rows_before(rows, halo_ref, branch, lanes)
            taps = [jnp.broadcast_to(taps_ref[branch, j : j + 1, lanes], (SEGS, LANES)) for j in range(TAPS)]
            for t in range(STEPS):
                total = taps[0] * rows[t]
                for j in range(1, TAPS):
                    earlier = rows[t - j] if t >= j else before[t - j]
                    total = total + taps[j] * (earlier * masks[j - 1, t])
                feat_ref[tile, slab(branch, t)] = total
        for t in range(STEPS):
            pre_ref[tile, slab(SOURCE, t)] = feat_ref[tile, slab(1, t)] * feat_ref[tile, slab(2, t)]
            pre_ref[tile, slab(GRAD, t)] = raw_ref[tile, slab(COT, t)] * feat_ref[tile, slab(0, t)]
        for low in range(0, MODES, 8):
            modes = range(low, low + 8)
            decay = [row(decay_ref, m, lanes) for m in modes]
            ends = [pre_ref[tile, slab(SOURCE, 0)] * end_mask[0]] * 8
            for t in range(1, STEPS):
                value = pre_ref[tile, slab(SOURCE, t)] * end_mask[t]
                ends = [d * e + value for d, e in zip(decay, ends)]
            begins = [pre_ref[tile, slab(GRAD, STEPS - 1)] * open_mask[STEPS - 1]] * 8
            for t in range(STEPS - 2, -1, -1):
                value = pre_ref[tile, slab(GRAD, t)] * open_mask[t]
                begins = [d * b + value for d, b in zip(decay, begins)]
            for m, d, e, b in zip(modes, decay, ends, begins):
                pre_ref[tile, slab(GSEG, m)] = b
                for _ in range(4):
                    d = d * d
                for k in range(3):
                    e = e + (d * chain[k]) * pltpu.roll(e, 1 << k, 0)
                    b = b + (d * chain[3 + k]) * pltpu.roll(b, SEGS - (1 << k), 0)
                    d = d * d
                pre_ref[tile, slab(SLOC, m)] = jnp.where(first, 0.0, pltpu.roll(e, 1, 0))
                pre_ref[tile, slab(RLOC, m)] = jnp.where(last, 0.0, pltpu.roll(b, SEGS - 1, 0))
                own_ref[m : m + 1, lanes] = jnp.where(lower, e[SEGS - 1 :], b[:1])
                sent_ref[m : m + 1, lanes] = jnp.where(lower, b[:1], e[SEGS - 1 :])
        power = jnp.exp(rate_ref[:, lanes] * -float(ROWS))
        pass_ref[0, :, lanes] = own_pass * power
        pass_ref[1, :, lanes] = partner_pass * power
        power = power * power
        pass_ref[2, :, lanes] = chip_pass * power
        pass_ref[3, :, lanes] = far_pass * (power * power)

    each_tile(raw_ref.shape[0], tile_body)


def local_kernel(
    spot_ref, pre_ref, rate_ref, decay_ref, residue_ref, skip_ref, open_mask, end_mask,
    post_ref, local_ref, first_ref,
    masks, reach, stage, weight_stage,
):
    starts, anchor = starts_of(spot_ref), spot_ref[0] * ROWS

    store_masks(starts, anchor, masks, STEPS, STEPS - 1)
    before = since_start(starts, anchor + segments() * STEPS - 1)
    reach[0] = flag((before >= segments() * STEPS) | (segments() == 0))
    at_end = since_start(starts, anchor + segments() * 0 + ROWS - 1)
    reach[1] = flag(at_end >= (SEGS - 1 - segments()) * STEPS)

    def tile_body(tile, lanes):
        segment = segments().astype(F32)
        rates = rate_ref[:, lanes]
        decay = decay_ref[:, lanes]
        power = residue_ref[:, lanes] * jnp.sqrt(rates)
        weight_stage[...] = power * decay
        kernel = []
        for gap in range(STEPS):
            kernel.append(jnp.sum(power, axis=0, keepdims=True))
            power = power * decay
        kernel[0] = kernel[0] + skip_ref[:, lanes]
        source = [pre_ref[tile, slab(SOURCE, t)] for t in range(STEPS)]
        grads = [pre_ref[tile, slab(GRAD, t)] for t in range(STEPS)]
        conv, back, paired = [None] * STEPS, [None] * STEPS, []
        for gap in range(STEPS):
            weight = jnp.broadcast_to(kernel[gap], (SEGS, LANES))
            pair = jnp.zeros((SEGS, LANES), F32)
            for t in range(gap, STEPS):
                value, grad = source[t - gap], grads[t]
                if gap:
                    value, grad = value * masks[gap - 1, t], grad * masks[gap - 1, t]
                conv[t] = weight * value if gap == 0 else conv[t] + weight * value
                back[t - gap] = weight * grad if gap == 0 else back[t - gap] + weight * grad
                pair = pair + grads[t] * value
            paired.append(jnp.sum(pair, axis=0, keepdims=True))
        for t in range(STEPS):
            post_ref[tile, slab(CONV, t)] = conv[t]
            post_ref[tile, slab(BACK, t)] = back[t]
        scaled = [weight_stage[...]]
        for t in range(1, STEPS):
            scaled.append(scaled[-1] * decay)
        later = pre_ref[tile, pl.ds(RLOC * ROWS, MODES, stride=SEGS), :]
        beyond = reach[1, :1] * jnp.exp(rates * -float(ROWS - STEPS))
        for t in range(HALO):
            far_term = end_mask[t, :1] * scaled[STEPS - 1 - t]
            first_ref[tile, NEAR_TERMS + t * MODES : NEAR_TERMS + (t + 1) * MODES] = open_mask[t, :1] * scaled[t]
            first_ref[tile, FAR_TERMS + t * MODES : FAR_TERMS + (t + 1) * MODES] = far_term * beyond
            back_row = back[t][:1] + jnp.sum(far_term * later, axis=0, keepdims=True)
            first_ref[tile, CONV_ROWS + t : CONV_ROWS + t + 1] = conv[t][:1]
            first_ref[tile, BACK_ROWS + t : BACK_ROWS + t + 1] = back_row
        total = jnp.broadcast_to(paired[STEPS - 1], (MODES, LANES))
        for gap in range(STEPS - 2, -1, -1):
            total = total * decay + paired[gap]
        for m in range(MODES):
            arriving = pre_ref[tile, slab(SLOC, m)]
            stage[m : m + 1, :] = jnp.sum(arriving * pre_ref[tile, slab(GSEG, m)], axis=0, keepdims=True)
            scale = row(weight_stage, m, slice(None))
            rate = row(rate_ref, m, lanes) * (-float(STEPS))
            post_ref[tile, slab(SWT, m)] = scale * arriving
            post_ref[tile, slab(RWT, m)] = scale * pre_ref[tile, slab(RLOC, m)]
            post_ref[tile, slab(SCOEF, m)] = scale * reach[0] * jnp.exp(rate * segment)
            post_ref[tile, slab(RCOEF, m)] = scale * reach[1] * jnp.exp(rate * (SEGS - 1 - segment))
        local_ref[tile, 0:MODES] = total + stage[...] * decay
        local_ref[tile, MODES : MODES + 8] = jnp.broadcast_to(paired[0], (8, LANES))

    each_tile(pre_ref.shape[0], tile_body)


def tree_sum(values):
    while len(values) > 1:
        values = [a + b for a, b in zip(values[::2], values[1::2])]
    return values[0]


def tile_slot(tile, spot_ref):
    core, place = spot_ref[0] % 2, spot_ref[1]
    half = jnp.where(tile // 8 == core, 0, 1)
    slot = tile % 8
    high, low = slot // 4, (slot // 2) % 2
    high = jnp.where(high == place // 2, 0, 1)
    low = jnp.where(low == place % 2, 0, 1)
    return half, high * 4 + low * 2 + slot % 2


def edge_kernel(
    spot_ref, raw_ref, feat_ref, first_ref, arrived_ref, handed_ref, enter_ref, return_ref, edge_ref
):
    lower = spot_ref[0] % 2 == 0

    def tile_body(tile, lanes):
        arrived, handed = arrived_ref[:, lanes], handed_ref[:, lanes]
        entering, returning = jnp.where(lower, arrived, handed), jnp.where(lower, handed, arrived)
        enter_ref[:, lanes] = entering
        return_ref[:, lanes] = returning
        for t in range(HALO):
            near = first_ref[tile, NEAR_TERMS + t * MODES : NEAR_TERMS + (t + 1) * MODES]
            far = first_ref[tile, FAR_TERMS + t * MODES : FAR_TERMS + (t + 1) * MODES]
            filtered = first_ref[tile, CONV_ROWS + t : CONV_ROWS + t + 1]
            filtered = filtered + jnp.sum(near * entering, axis=0, keepdims=True)
            grad = first_ref[tile, BACK_ROWS + t : BACK_ROWS + t + 1]
            grad = grad + jnp.sum(far * returning, axis=0, keepdims=True)
            edge_ref[t : t + 1, lanes] = raw_ref[tile, slab(COT, t)][:1] * filtered
            edge_ref[8 + t : 9 + t, lanes] = grad * feat_ref[tile, slab(2, t)][:1]
            edge_ref[16 + t : 17 + t, lanes] = grad * feat_ref[tile, slab(1, t)][:1]
        for branch in range(3):
            edge_ref[branch * 8 + HALO : branch * 8 + 8, lanes] = jnp.zeros((8 - HALO, LANES), F32)

    each_tile(raw_ref.shape[0], tile_body)


def gradient_kernel(
    spot_ref, raw_ref, feat_ref, post_ref, local_ref, enter_ref, return_ref, own_ref, sent_ref, rate_ref, decay_ref, halo_ref,
    masks, open_mask, end_mask,
    out_ref, gfeat_ref, kept_ref, away_ref,
    stage,
):
    lower = spot_ref[0] % 2 == 0

    def tile_body(tile, lanes):
        decay = [row(decay_ref, m, lanes) for m in range(MODES)]
        state = [
            post_ref[tile, slab(SWT, m)] + post_ref[tile, slab(SCOEF, m)] * row(enter_ref, m, lanes)
            for m in range(MODES)
        ]
        for t in range(STEPS):
            filtered = post_ref[tile, slab(CONV, t)] + open_mask[t] * tree_sum(state)
            stage[pl.ds(t, SEGS, stride=STEPS), :] = feat_ref[tile, slab(0, t)] * filtered
            gfeat_ref[tile, slab(0, t)] = raw_ref[tile, slab(COT, t)] * filtered
            if t < STEPS - 1:
                state = [d * s for d, s in zip(decay, state)]
        out_ref[:, lanes] = stage[...].astype(out_ref.dtype)
        state = [
            post_ref[tile, slab(RWT, m)] + post_ref[tile, slab(RCOEF, m)] * row(return_ref, m, lanes)
            for m in range(MODES)
        ]
        for t in range(STEPS - 1, -1, -1):
            grad = post_ref[tile, slab(BACK, t)] + end_mask[t] * tree_sum(state)
            gfeat_ref[tile, slab(1, t)] = grad * feat_ref[tile, slab(2, t)]
            gfeat_ref[tile, slab(2, t)] = grad * feat_ref[tile, slab(1, t)]
            if t:
                state = [d * s for d, s in zip(decay, state)]
        rates = rate_ref[:, lanes]
        begin = jnp.where(lower, sent_ref[:, lanes], own_ref[:, lanes])
        sums = [jnp.sqrt(rates) * (local_ref[tile, 0:MODES] + enter_ref[:, lanes] * decay_ref[:, lanes] * begin)]
        for branch in range(3):
            totals = [jnp.zeros((SEGS, LANES), F32)] * TAPS
            rows = [raw_ref[tile, slab(branch, t)] for t in range(STEPS)]
            before = rows_before(rows, halo_ref, branch, lanes)
            for t in range(STEPS):
                grad = gfeat_ref[tile, slab(branch, t)]
                totals[0] = totals[0] + grad * rows[t]
                for j in range(1, TAPS):
                    earlier = rows[t - j] if t >= j else before[t - j]
                    totals[j] = totals[j] + (grad * masks[j - 1, t]) * earlier
            sums += [jnp.sum(total, axis=0, keepdims=True) for total in totals]
        sums.append(local_ref[tile, MODES : MODES + REDUCED - MODES - 3 * TAPS])
        half, slot = tile_slot(tile, spot_ref)
        for which, ref in enumerate((kept_ref, away_ref)):

            @pl.when(half == which)
            def _(ref=ref):
                at = 0
                for piece in sums:
                    ref[slot, at : at + piece.shape[0]] = piece
                    at += piece.shape[0]

    each_tile(raw_ref.shape[0], tile_body)


def input_kernel(branch, gfeat_ref, edge_ref, taps_ref, masks, out_ref, stage):

    def tile_body(tile, lanes):
        last = segments() == SEGS - 1
        rows = [gfeat_ref[tile, slab(branch, t)] for t in range(STEPS)]
        for t in range(HALO):
            edge = row(edge_ref, branch * 8 + t, lanes)
            rows.append(jnp.where(last, edge, pltpu.roll(rows[t], SEGS - 1, 0)))
        taps = [jnp.broadcast_to(taps_ref[branch, j : j + 1, lanes], (SEGS, LANES)) for j in range(TAPS)]
        for t in range(STEPS):
            total = taps[0] * rows[t]
            for j in range(1, TAPS):
                total = total + taps[j] * (rows[t + j] * masks[j - 1, t + j])
            stage[pl.ds(t, SEGS, stride=STEPS), :] = total
        out_ref[:, lanes] = stage[...].astype(out_ref.dtype)

    each_tile(gfeat_ref.shape[0], tile_body)


def result_kernel(spot_ref, kept_ref, away_ref, short_ref, residue_ref, skip_ref):
    def tile_body(tile, lanes):
        half, slot = tile_slot(tile, spot_ref)
        block = jnp.where(half == 0, kept_ref[slot], away_ref[slot])
        for branch in range(3):
            at = MODES + branch * TAPS
            short_ref[branch, :, lanes] = block[at : at + TAPS]
        residue_ref[:, lanes] = block[:MODES]
        at = MODES + 3 * TAPS
        skip_ref[:, lanes] = block[at : at + 1]

    each_tile(kept_ref.shape[0] * 2, tile_body)


def combine_kernel(which, first_ref, pass_ref, second_ref, out_ref):
    out_ref[...] = first_ref[...] + pass_ref[which] * second_ref[...]


def arrive_kernel(near_ref, far_ref, own_ref, pass_ref, arrived_ref, handed_ref):
    arrived_ref[...] = near_ref[...] + pass_ref[3] * far_ref[...]
    handed_ref[...] = own_ref[...] + pass_ref[0] * arrived_ref[...]


SMEM, VMEM, HBM = (pl.BlockSpec(memory_space=space) for space in (pltpu.SMEM, pltpu.VMEM, pltpu.HBM))
MASKS = (HALO, STEPS + HALO, SEGS, LANES)
EDGE_MASKS = (STEPS, SEGS, LANES)
STAGE = (ROWS, LANES)


def call(body, name, ins, outs, scratch, *args, dtype=F32):
    return pl.pallas_call(
        body,
        name=name,
        out_shape=[out if isinstance(out, jax.ShapeDtypeStruct) else pltpu.VMEM(out, dtype) for out in outs],
        in_specs=ins,
        out_specs=[VMEM] * len(outs),
        scratch_shapes=[pltpu.VMEM(one, F32) if isinstance(one, tuple) else one for one in scratch],
        compiler_params=pltpu.CompilerParams(vmem_limit_bytes=VMEM_BYTES),
        cost_estimate=pl.CostEstimate(flops=1 << 26, bytes_accessed=8 << 20, transcendentals=0),
    )(*[x if spec is SMEM else pltpu.with_memory_space_constraint(x, spec.memory_space) for x, spec in zip(args, ins)])


def tails(query, key, value):
    [made] = call(
        tail_kernel, "last_rows", [HBM] * 3, [(32, query.shape[1])],
        [pltpu.VMEM((3, 16, query.shape[1]), BF16), pltpu.SemaphoreType.DMA((3,))],
        query, key, value, dtype=BF16,
    )
    return made


def staged(place, lengths, query, key, value, upstream, taps, rate, residue, skip):
    channels = query.shape[1]
    return call(
        stage_kernel, "stage",
        [SMEM] + [HBM] * 9,
        [(channels // LANES, 4 * ROWS, LANES), MASKS, EDGE_MASKS, EDGE_MASKS, (6, SEGS, LANES),
         taps.shape, rate.shape, residue.shape, skip.shape, rate.shape],
        [(4, *STAGE), pltpu.VMEM((4, ROWS, channels), BF16), pltpu.SemaphoreType.DMA((4, CHUNKS)),
         pltpu.SemaphoreType.DMA((4,)), pltpu.SMEM(lengths.shape, jnp.int32), pltpu.SemaphoreType.DMA],
        place, lengths, query, key, value, upstream, taps, rate, residue, skip,
    )


def features(spot, raw, masks, open_mask, end_mask, chain, taps, rate, decay, halo):
    tiles, states = raw.shape[0], rate.shape
    return call(
        feature_kernel, "features",
        [SMEM] + [VMEM] * 9,
        [(tiles, 3 * ROWS, LANES), (tiles, 5 * ROWS, LANES), states, states, (4, *states)],
        [],
        spot, raw, masks, open_mask, end_mask, chain, taps, rate, decay, halo,
    )


def local_filter(spot, pre, rate, decay, residue, skip, open_mask, end_mask):
    tiles = pre.shape[0]
    return call(
        local_kernel, "local_filter",
        [SMEM] + [VMEM] * 7,
        [(tiles, 6 * ROWS, LANES), (tiles, MODES + 8, LANES), (tiles, FIRST_ROWS, LANES)],
        [(STEPS - 1, STEPS, SEGS, LANES), (2, SEGS, LANES), (MODES, LANES), (MODES, LANES)],
        spot, pre, rate, decay, residue, skip, open_mask, end_mask,
    )


def edge_gradients(spot, raw, feat, first, arrived, handed):
    states = arrived.shape
    return call(
        edge_kernel, "edge_gradients", [SMEM] + [VMEM] * 5, [states, states, (24, states[1])], [],
        spot, raw, feat, first, arrived, handed,
    )


def filter_gradients(spot, raw, *others):
    tiles = raw.shape[0]
    half = (tiles // 2, REDUCED, LANES)
    return call(
        gradient_kernel, "filter_gradients",
        [SMEM] + [VMEM] * (1 + len(others)),
        [jax.ShapeDtypeStruct((ROWS, tiles * LANES), BF16), (tiles, 3 * ROWS, LANES), half, half],
        [STAGE],
        spot, raw, *others,
    )


def input_gradient(branch, gfeat, edge, taps, masks):
    [made] = call(
        partial(input_kernel, branch), "input_gradient",
        [VMEM] * 4,
        [jax.ShapeDtypeStruct((ROWS, taps.shape[2]), BF16)],
        [STAGE],
        gfeat, edge, taps, masks,
    )
    return made


def results(spot, kept, away):
    channels = 2 * kept.shape[0] * LANES
    shapes = (3, TAPS, channels), (MODES, channels), (1, channels)
    return call(
        result_kernel, "parameter_gradients",
        [SMEM, VMEM, VMEM], [jax.ShapeDtypeStruct(shape, F32) for shape in shapes], [], spot, kept, away,
    )


def combine(which, first, through, second):
    [made] = call(
        partial(combine_kernel, which), "combine", [VMEM] * 3, [first.shape], [], first, through, second
    )
    return made


def per_device(query_rows, key_rows, value_rows, cotangent, lengths, short_filter, residue, decay_rate, skip_gain):
    count = lax.axis_size("ctx")
    place = jnp.stack([lax.axis_index("ctx"), lax.axis_index("dp")]).astype(jnp.int32)
    spot = jnp.concatenate([place, lengths[0]])

    halo = lax.ppermute(tails(query_rows[0], key_rows[0], value_rows[0]), "ctx", [(i, i + 1) for i in range(count - 1)]).astype(F32)
    raw, masks, open_mask, end_mask, chain, taps, rate, residue, skip, decay = staged(
        place, lengths, query_rows[0], key_rows[0], value_rows[0], cotangent[0],
        short_filter, decay_rate.T, residue.T, skip_gain[None],
    )
    feat, pre, own, sent, through = features(spot, raw, masks, open_mask, end_mask, chain, taps, rate, decay, halo)

    pairs = [(i, i ^ 1) for i in range(count)]

    def onward(value, chips):
        moves = [(i, i + 2 * chips * (1 - 2 * (i % 2))) for i in range(count)]
        return lax.ppermute(value, "ctx", [(i, j) for i, j in moves if 0 <= j < count])

    chip_state = combine(1, lax.ppermute(sent, "ctx", pairs), through, own)
    chip_state = combine(2, chip_state, through, onward(chip_state, 1))
    chip_state, pre = lax.optimization_barrier((chip_state, pre))
    near, far = onward(chip_state, 1), onward(chip_state, 3)
    post, local, first = local_filter(spot, pre, rate, decay, residue, skip, open_mask, end_mask)
    far, post = lax.optimization_barrier((far, post))
    arrived, handed = call(
        arrive_kernel, "arrive", [VMEM] * 4, [own.shape, own.shape], [], near, far, own, through
    )
    handed = lax.ppermute(handed, "ctx", pairs)

    entering, returning, edge = edge_gradients(spot, raw, feat, first, arrived, handed)
    next_edge = lax.ppermute(edge, "ctx", [(i, i - 1) for i in range(1, count)])
    block_out, gfeat, kept, away = filter_gradients(
        spot, raw, feat, post, local, entering, returning, own, sent, rate, decay, halo, masks, open_mask, end_mask
    )
    away, next_edge = lax.optimization_barrier((away, next_edge))

    def exchange(value, axis, flip):
        return lax.ppermute(value, axis, [(i, i ^ flip) for i in range(lax.axis_size(axis))])

    grad_inputs = []

    def exchanges(sent, axis, flips, beside=True):
        if not beside:
            return [exchange(value, axis, flip) for value, flip in zip(sent, flips)]
        *sent, edge_now = lax.optimization_barrier((*sent, next_edge))
        made = input_gradient(len(grad_inputs), gfeat, edge_now, taps, masks)
        *received, made = lax.optimization_barrier((*exchanges(sent, axis, flips, False), made))
        grad_inputs.append(made)
        return received

    total = kept + exchange(away, "ctx", 1)
    quarter = total.shape[0] // 4
    quarters = [total[quarter * i : quarter * (i + 1)] for i in range(4)]
    one, two, three = exchanges(quarters[1:], "dp", (1, 2, 3), False)
    total = (quarters[0] + one) + (two + three)
    total = total + exchanges([total], "ctx", (2,))[0]
    one, two, three = exchanges([total] * 3, "ctx", (4, 8, 12))
    total = (total + one) + (two + three)
    total = jnp.concatenate([total, *exchanges([total] * 3, "dp", (1, 2, 3))])
    grad_short, grad_residue, grad_skip = results(spot, total, exchange(total, "ctx", 1))
    return (block_out[None], *(g[None] for g in grad_inputs), grad_short, grad_residue.T, grad_skip[0])


def solution(mesh):
    rows = P("dp", "ctx", "ch")
    return jax.shard_map(
        per_device,
        mesh=mesh,
        in_specs=(rows, rows, rows, rows, P("dp", None), P(None, None, "ch"), P("ch", None), P("ch", None), P("ch")),
        out_specs=(rows, rows, rows, rows, P(None, None, "ch"), P("ch", None), P("ch")),
        check_vma=False,
    )
```

```python
from functools import partial

import jax
import jax.numpy as jnp
from jax import lax
from jax.experimental import pallas as pl
from jax.experimental.pallas import tpu as pltpu
from jax.sharding import PartitionSpec as P

SEGS = 8
STEPS = 16
ROWS = SEGS * STEPS
TAPS = 7
HALO = TAPS - 1
MODES = 16
LANES = 128
REDUCED = 40
F32 = jnp.float32
BF16 = jnp.bfloat16
VMEM_BYTES = 12 << 20
CHUNKS = 4
COT = 3
SOURCE, GRAD, GSEG, SLOC, RLOC = range(5)
CONV, BACK = range(2)
SWT, RWT, SCOEF, RCOEF = range(4)


def slab(block, index):
    at = block * ROWS + index * SEGS
    return slice(at, at + SEGS)


def row(ref, index, lanes):
    return jnp.broadcast_to(ref[index : index + 1, lanes], (SEGS, LANES))


def starts_of(spot_ref):
    return sums_before([spot_ref[j] for j in range(2, spot_ref.shape[0])])


def sums_before(lengths):
    found = [jnp.int32(0)]
    for length in lengths[:-1]:
        found.append(found[-1] + length)
    return found


def since_start(starts, positions):
    begun = jnp.zeros_like(positions)
    for start in starts:
        begun = jnp.where(positions >= start, start, begun)
    return positions - begun


def segments():
    return lax.broadcasted_iota(jnp.int32, (SEGS, LANES), 0)


def flag(condition):
    return jnp.where(condition, 1.0, 0.0)


def store_masks(starts, anchor, mask_ref, steps, gaps):
    for t in range(steps):
        dist = since_start(starts, anchor + segments() * STEPS + t)
        for gap in range(1, gaps + 1):
            mask_ref[gap - 1, t] = flag(dist >= gap)


def store_edge_masks(starts, anchor, open_mask, end_mask):
    at_end = since_start(starts, anchor + segments() * STEPS + STEPS - 1)
    for t in range(STEPS):
        dist = since_start(starts, anchor + segments() * STEPS + t)
        open_mask[t] = flag(dist >= t + 1)
        end_mask[t] = flag(at_end >= STEPS - 1 - t)


def each_tile(count, body):
    def step(index, carry):
        body(index, pl.ds(pl.multiple_of(index * LANES, LANES), LANES))
        return carry

    lax.fori_loop(0, count, step, 0)


def fetch_columns(ref, stage, lanes):
    stage[...] = ref[:, lanes].astype(F32)
    return [stage[pl.ds(t, SEGS, stride=STEPS), :] for t in range(STEPS)]


def rows_before(rows, halo_ref, branch, lanes):
    first = segments() == 0
    return {
        -back: jnp.where(first, row(halo_ref, branch * 8 + 8 - back, lanes), pltpu.roll(rows[STEPS - back], 1, 0))
        for back in range(1, HALO + 1)
    }


def tail_kernel(q_ref, k_ref, v_ref, out_ref, rows, arrived):
    copies = [
        pltpu.make_async_copy(ref.at[ROWS - 16 :], rows.at[which], arrived.at[which])
        for which, ref in enumerate((q_ref, k_ref, v_ref))
    ]
    for copy in copies:
        copy.start()
    for copy in copies:
        copy.wait()

    def tile_body(tile, lanes):
        q, k, v = (rows[which, :, lanes].astype(F32)[8:] for which in range(3))
        out_ref[0:16, lanes] = jnp.concatenate([q, k], axis=0).astype(BF16)
        out_ref[16:32, lanes] = jnp.concatenate([v, jnp.zeros_like(v)], axis=0).astype(BF16)

    each_tile(out_ref.shape[1] // LANES, tile_body)


def stage_kernel(
    place_ref, lengths_in, q_ref, k_ref, v_ref, cot_ref, taps_in, rate_in, residue_in, skip_in,
    raw_ref, masks, open_mask, end_mask, chain, taps_ref, rate_ref, residue_ref, skip_ref, decay_ref,
    stage, columns, arrived, loaded, lengths_ref, known,
):
    inputs = (q_ref, k_ref, v_ref, cot_ref)
    chunk = columns.shape[2] // CHUNKS
    anchor = place_ref[0] * ROWS
    lengths = pltpu.make_async_copy(lengths_in, lengths_ref, known)
    lengths.start()

    def fetch(which, part):
        cols = pl.ds(pl.multiple_of(part * chunk, LANES), chunk)
        return pltpu.make_async_copy(inputs[which].at[:, cols], columns.at[which, :, cols], arrived.at[which, part])

    parameters = [
        pltpu.make_async_copy(source, target, loaded.at[which])
        for which, (source, target) in enumerate(
            ((taps_in, taps_ref), (rate_in, rate_ref), (residue_in, residue_ref), (skip_in, skip_ref))
        )
    ]
    for part in range(CHUNKS):
        for which in range(4):
            fetch(which, part).start()
    for copy in parameters:
        copy.start()
    lengths.wait()
    starts = sums_before([lengths_ref[0, j] for j in range(lengths_ref.shape[1])])
    store_masks(starts, anchor, masks, STEPS + HALO, HALO)
    store_edge_masks(starts, anchor, open_mask, end_mask)
    for k in range(3):
        span = STEPS << k
        at_end = since_start(starts, anchor + segments() * STEPS + STEPS - 1)
        chain[k] = flag((at_end >= span) & (segments() >= (1 << k)))
        ahead = jnp.minimum(segments() + (1 << k), SEGS)
        at_end = since_start(starts, anchor + ahead * STEPS - 1)
        chain[3 + k] = flag((at_end >= span) & (segments() + (1 << k) < SEGS))

    def tile_body(tile, lanes):
        @pl.when(tile % (chunk // LANES) == 0)
        def _():
            for which in range(4):
                fetch(which, tile // (chunk // LANES)).wait()

        for which in range(4):
            rows = fetch_columns(columns.at[which], stage.at[which], lanes)
            for t in range(STEPS):
                raw_ref[tile, slab(which, t)] = rows[t]

    each_tile(raw_ref.shape[0], tile_body)
    for copy in parameters:
        copy.wait()

    def decay_body(tile, lanes):
        decay_ref[:, lanes] = jnp.exp(-rate_ref[:, lanes])

    each_tile(raw_ref.shape[0], decay_body)


def feature_kernel(
    spot_ref, raw_ref, masks, open_mask, end_mask, chain, taps_ref, rate_ref, decay_ref, halo_ref,
    feat_ref, pre_ref, own_ref, sent_ref, pass_ref,
):
    starts, here = starts_of(spot_ref), spot_ref[0]
    anchor, core, chip = here * ROWS, here % 2, here // 2

    def passes(position, span):
        return flag(since_start(starts, position) >= span)

    far_end = jnp.where(core == 0, chip, chip + 3) * 2 * ROWS - 1
    own_pass = passes(anchor + ROWS - 1, ROWS)
    partner_pass = passes((here + 1 - 2 * core) * ROWS + ROWS - 1, ROWS)
    chip_pass = passes(chip * 2 * ROWS + 2 * ROWS - 1, 2 * ROWS)
    far_pass = passes(far_end, 4 * ROWS)
    lower = core == 0

    def tile_body(tile, lanes):
        segment = segments()
        first, last = segment == 0, segment == SEGS - 1
        for branch in range(3):
            rows = [raw_ref[tile, slab(branch, t)] for t in range(STEPS)]
            before = rows_before(rows, halo_ref, branch, lanes)
            taps = [jnp.broadcast_to(taps_ref[branch, j : j + 1, lanes], (SEGS, LANES)) for j in range(TAPS)]
            for t in range(STEPS):
                total = taps[0] * rows[t]
                for j in range(1, TAPS):
                    earlier = rows[t - j] if t >= j else before[t - j]
                    total = total + taps[j] * (earlier * masks[j - 1, t])
                feat_ref[tile, slab(branch, t)] = total
        for t in range(STEPS):
            pre_ref[tile, slab(SOURCE, t)] = feat_ref[tile, slab(1, t)] * feat_ref[tile, slab(2, t)]
            pre_ref[tile, slab(GRAD, t)] = raw_ref[tile, slab(COT, t)] * feat_ref[tile, slab(0, t)]
        for low in range(0, MODES, 8):
            modes = range(low, low + 8)
            decay = [row(decay_ref, m, lanes) for m in modes]
            ends = [pre_ref[tile, slab(SOURCE, 0)] * end_mask[0]] * 8
            for t in range(1, STEPS):
                value = pre_ref[tile, slab(SOURCE, t)] * end_mask[t]
                ends = [d * e + value for d, e in zip(decay, ends)]
            begins = [pre_ref[tile, slab(GRAD, STEPS - 1)] * open_mask[STEPS - 1]] * 8
            for t in range(STEPS - 2, -1, -1):
                value = pre_ref[tile, slab(GRAD, t)] * open_mask[t]
                begins = [d * b + value for d, b in zip(decay, begins)]
            for m, d, e, b in zip(modes, decay, ends, begins):
                pre_ref[tile, slab(GSEG, m)] = b
                for _ in range(4):
                    d = d * d
                for k in range(3):
                    e = e + (d * chain[k]) * pltpu.roll(e, 1 << k, 0)
                    b = b + (d * chain[3 + k]) * pltpu.roll(b, SEGS - (1 << k), 0)
                    d = d * d
                pre_ref[tile, slab(SLOC, m)] = jnp.where(first, 0.0, pltpu.roll(e, 1, 0))
                pre_ref[tile, slab(RLOC, m)] = jnp.where(last, 0.0, pltpu.roll(b, SEGS - 1, 0))
                own_ref[m : m + 1, lanes] = jnp.where(lower, e[SEGS - 1 :], b[:1])
                sent_ref[m : m + 1, lanes] = jnp.where(lower, b[:1], e[SEGS - 1 :])
        power = jnp.exp(rate_ref[:, lanes] * -float(ROWS))
        pass_ref[0, :, lanes] = own_pass * power
        pass_ref[1, :, lanes] = partner_pass * power
        power = power * power
        pass_ref[2, :, lanes] = chip_pass * power
        pass_ref[3, :, lanes] = far_pass * (power * power)

    each_tile(raw_ref.shape[0], tile_body)


def segment_kernel(
    spot_ref, pre_ref, rate_ref, decay_ref, residue_ref, skip_ref,
    near_ref, pair_ref,
    masks,
):
    store_masks(starts_of(spot_ref), spot_ref[0] * ROWS, masks, STEPS, STEPS - 1)

    def tile_body(tile, lanes):
        decay = decay_ref[:, lanes]
        power = residue_ref[:, lanes] * jnp.sqrt(rate_ref[:, lanes])
        kernel = []
        for gap in range(STEPS):
            kernel.append(jnp.sum(power, axis=0, keepdims=True))
            power = power * decay
        kernel[0] = kernel[0] + skip_ref[:, lanes]
        source = [pre_ref[tile, slab(SOURCE, t)] for t in range(STEPS)]
        grads = [pre_ref[tile, slab(GRAD, t)] for t in range(STEPS)]
        conv, back = [None] * STEPS, [None] * STEPS
        for gap in range(STEPS):
            weight = jnp.broadcast_to(kernel[gap], (SEGS, LANES))
            pair = jnp.zeros((SEGS, LANES), F32)
            for t in range(gap, STEPS):
                value, grad = source[t - gap], grads[t]
                if gap:
                    value, grad = value * masks[gap - 1, t], grad * masks[gap - 1, t]
                conv[t] = weight * value if gap == 0 else conv[t] + weight * value
                back[t - gap] = weight * grad if gap == 0 else back[t - gap] + weight * grad
                pair = pair + grads[t] * value
            pair_ref[tile, gap : gap + 1] = jnp.sum(pair, axis=0, keepdims=True)
        for t in range(STEPS):
            near_ref[tile, slab(CONV, t)] = conv[t]
            near_ref[tile, slab(BACK, t)] = back[t]

    each_tile(pre_ref.shape[0], tile_body)


def local_kernel(
    spot_ref, pre_ref, pair_ref, rate_ref, decay_ref, residue_ref,
    post_ref, local_ref,
    reach, stage, weight_stage,
):
    starts, anchor = starts_of(spot_ref), spot_ref[0] * ROWS
    before = since_start(starts, anchor + segments() * STEPS - 1)
    reach[0] = flag((before >= segments() * STEPS) | (segments() == 0))
    at_end = since_start(starts, anchor + segments() * 0 + ROWS - 1)
    reach[1] = flag(at_end >= (SEGS - 1 - segments()) * STEPS)

    def tile_body(tile, lanes):
        segment = segments().astype(F32)
        rates = rate_ref[:, lanes]
        decay = decay_ref[:, lanes]
        weight_stage[...] = residue_ref[:, lanes] * jnp.sqrt(rates) * decay
        total = jnp.broadcast_to(pair_ref[tile, STEPS - 1 : STEPS], (MODES, LANES))
        for gap in range(STEPS - 2, -1, -1):
            total = total * decay + pair_ref[tile, gap : gap + 1]
        for m in range(MODES):
            arriving = pre_ref[tile, slab(SLOC, m)]
            stage[m : m + 1, :] = jnp.sum(arriving * pre_ref[tile, slab(GSEG, m)], axis=0, keepdims=True)
            scale = row(weight_stage, m, slice(None))
            rate = row(rate_ref, m, lanes) * (-float(STEPS))
            post_ref[tile, slab(SWT, m)] = scale * arriving
            post_ref[tile, slab(RWT, m)] = scale * pre_ref[tile, slab(RLOC, m)]
            post_ref[tile, slab(SCOEF, m)] = scale * reach[0] * jnp.exp(rate * segment)
            post_ref[tile, slab(RCOEF, m)] = scale * reach[1] * jnp.exp(rate * (SEGS - 1 - segment))
        local_ref[tile, 0:MODES] = total + stage[...] * decay
        local_ref[tile, MODES : MODES + 8] = jnp.broadcast_to(pair_ref[tile, 0:1], (8, LANES))

    each_tile(pre_ref.shape[0], tile_body)


def tree_sum(values):
    while len(values) > 1:
        values = [a + b for a, b in zip(values[::2], values[1::2])]
    return values[0]


def tile_slot(tile, spot_ref):
    core, place = spot_ref[0] % 2, spot_ref[1]
    half = jnp.where(tile // 8 == core, 0, 1)
    slot = tile % 8
    high, low = slot // 4, (slot // 2) % 2
    high = jnp.where(high == place // 2, 0, 1)
    low = jnp.where(low == place % 2, 0, 1)
    return half, high * 4 + low * 2 + slot % 2


def gradient_kernel(
    spot_ref, raw_ref, feat_ref, near_ref, post_ref, local_ref, arrived_ref, handed_ref, own_ref, sent_ref, rate_ref, decay_ref, halo_ref,
    masks, open_mask, end_mask,
    out_ref, gfeat_ref, edge_ref, kept_ref, away_ref,
    stage, rounded, written, states,
):
    lower = spot_ref[0] % 2 == 0

    chunk = rounded.shape[1] // CHUNKS

    def write(part):
        cols = pl.ds(pl.multiple_of(part * chunk, LANES), chunk)
        return pltpu.make_async_copy(rounded.at[:, cols], out_ref.at[:, cols], written.at[part])

    def tile_body(tile, lanes):
        decay = [row(decay_ref, m, lanes) for m in range(MODES)]
        arrived, handed = arrived_ref[:, lanes], handed_ref[:, lanes]
        entering = jnp.where(lower, arrived, handed)
        states[0:MODES] = entering
        states[MODES:] = jnp.where(lower, handed, arrived)
        state = [
            post_ref[tile, slab(SWT, m)] + post_ref[tile, slab(SCOEF, m)] * row(states, m, slice(None))
            for m in range(MODES)
        ]
        for t in range(STEPS):
            filtered = near_ref[tile, slab(CONV, t)] + open_mask[t] * tree_sum(state)
            stage[pl.ds(t, SEGS, stride=STEPS), :] = feat_ref[tile, slab(0, t)] * filtered
            gfeat_ref[tile, slab(0, t)] = raw_ref[tile, slab(COT, t)] * filtered
            if t < STEPS - 1:
                state = [d * s for d, s in zip(decay, state)]
        rounded[:, lanes] = stage[...].astype(rounded.dtype)

        @pl.when(tile % (chunk // LANES) == chunk // LANES - 1)
        def _():
            write(tile // (chunk // LANES)).start()

        state = [
            post_ref[tile, slab(RWT, m)] + post_ref[tile, slab(RCOEF, m)] * row(states, MODES + m, slice(None))
            for m in range(MODES)
        ]
        for t in range(STEPS - 1, -1, -1):
            grad = near_ref[tile, slab(BACK, t)] + end_mask[t] * tree_sum(state)
            gfeat_ref[tile, slab(1, t)] = grad * feat_ref[tile, slab(2, t)]
            gfeat_ref[tile, slab(2, t)] = grad * feat_ref[tile, slab(1, t)]
            if t:
                state = [d * s for d, s in zip(decay, state)]
        rates = rate_ref[:, lanes]
        begin = jnp.where(lower, sent_ref[:, lanes], own_ref[:, lanes])
        sums = [jnp.sqrt(rates) * (local_ref[tile, 0:MODES] + entering * decay_ref[:, lanes] * begin)]
        for branch in range(3):
            totals = [jnp.zeros((SEGS, LANES), F32)] * TAPS
            rows = [raw_ref[tile, slab(branch, t)] for t in range(STEPS)]
            before = rows_before(rows, halo_ref, branch, lanes)
            for t in range(STEPS):
                grad = gfeat_ref[tile, slab(branch, t)]
                if t < HALO:
                    edge_ref[branch * 8 + t : branch * 8 + t + 1, lanes] = grad[:1]
                totals[0] = totals[0] + grad * rows[t]
                for j in range(1, TAPS):
                    earlier = rows[t - j] if t >= j else before[t - j]
                    totals[j] = totals[j] + (grad * masks[j - 1, t]) * earlier
            edge_ref[branch * 8 + HALO : branch * 8 + 8, lanes] = jnp.zeros((8 - HALO, LANES), F32)
            sums += [jnp.sum(total, axis=0, keepdims=True) for total in totals]
        sums.append(local_ref[tile, MODES : MODES + REDUCED - MODES - 3 * TAPS])
        half, slot = tile_slot(tile, spot_ref)
        for which, ref in enumerate((kept_ref, away_ref)):

            @pl.when(half == which)
            def _(ref=ref):
                at = 0
                for piece in sums:
                    ref[slot, at : at + piece.shape[0]] = piece
                    at += piece.shape[0]

    each_tile(raw_ref.shape[0], tile_body)
    for part in range(CHUNKS):
        write(part).wait()


def input_kernel(branch, gfeat_ref, edge_ref, taps_ref, masks, out_ref, stage):

    def tile_body(tile, lanes):
        last = segments() == SEGS - 1
        rows = [gfeat_ref[tile, slab(branch, t)] for t in range(STEPS)]
        for t in range(HALO):
            edge = row(edge_ref, branch * 8 + t, lanes)
            rows.append(jnp.where(last, edge, pltpu.roll(rows[t], SEGS - 1, 0)))
        taps = [jnp.broadcast_to(taps_ref[branch, j : j + 1, lanes], (SEGS, LANES)) for j in range(TAPS)]
        for t in range(STEPS):
            total = taps[0] * rows[t]
            for j in range(1, TAPS):
                total = total + taps[j] * (rows[t + j] * masks[j - 1, t + j])
            stage[pl.ds(t, SEGS, stride=STEPS), :] = total
        out_ref[:, lanes] = stage[...].astype(out_ref.dtype)

    each_tile(gfeat_ref.shape[0], tile_body)


def result_kernel(spot_ref, kept_ref, away_ref, short_ref, residue_ref, skip_ref):
    def tile_body(tile, lanes):
        half, slot = tile_slot(tile, spot_ref)
        block = jnp.where(half == 0, kept_ref[slot], away_ref[slot])
        for branch in range(3):
            at = MODES + branch * TAPS
            short_ref[branch, :, lanes] = block[at : at + TAPS]
        residue_ref[:, lanes] = block[:MODES]
        at = MODES + 3 * TAPS
        skip_ref[:, lanes] = block[at : at + 1]

    each_tile(kept_ref.shape[0] * 2, tile_body)


def combine_kernel(which, first_ref, pass_ref, second_ref, out_ref):
    out_ref[...] = first_ref[...] + pass_ref[which] * second_ref[...]


def arrive_kernel(near_ref, far_ref, own_ref, pass_ref, arrived_ref, handed_ref):
    arrived_ref[...] = near_ref[...] + pass_ref[3] * far_ref[...]
    handed_ref[...] = own_ref[...] + pass_ref[0] * arrived_ref[...]


SMEM, VMEM, HBM = (pl.BlockSpec(memory_space=space) for space in (pltpu.SMEM, pltpu.VMEM, pltpu.HBM))
MASKS = (HALO, STEPS + HALO, SEGS, LANES)
EDGE_MASKS = (STEPS, SEGS, LANES)
STAGE = (ROWS, LANES)


def call(body, name, ins, outs, scratch, *args, dtype=F32, specs=None):
    return pl.pallas_call(
        body,
        name=name,
        out_shape=[out if isinstance(out, jax.ShapeDtypeStruct) else pltpu.VMEM(out, dtype) for out in outs],
        in_specs=ins,
        out_specs=specs or [VMEM] * len(outs),
        scratch_shapes=[pltpu.VMEM(one, F32) if isinstance(one, tuple) else one for one in scratch],
        compiler_params=pltpu.CompilerParams(vmem_limit_bytes=VMEM_BYTES),
        cost_estimate=pl.CostEstimate(flops=1 << 26, bytes_accessed=8 << 20, transcendentals=0),
    )(*[x if spec is SMEM else pltpu.with_memory_space_constraint(x, spec.memory_space) for x, spec in zip(args, ins)])


def tails(query, key, value):
    [made] = call(
        tail_kernel, "last_rows", [HBM] * 3, [(32, query.shape[1])],
        [pltpu.VMEM((3, 16, query.shape[1]), BF16), pltpu.SemaphoreType.DMA((3,))],
        query, key, value, dtype=BF16,
    )
    return made


def staged(place, lengths, query, key, value, upstream, taps, rate, residue, skip):
    channels = query.shape[1]
    return call(
        stage_kernel, "stage",
        [SMEM] + [HBM] * 9,
        [(channels // LANES, 4 * ROWS, LANES), MASKS, EDGE_MASKS, EDGE_MASKS, (6, SEGS, LANES),
         taps.shape, rate.shape, residue.shape, skip.shape, rate.shape],
        [(4, *STAGE), pltpu.VMEM((4, ROWS, channels), BF16), pltpu.SemaphoreType.DMA((4, CHUNKS)),
         pltpu.SemaphoreType.DMA((4,)), pltpu.SMEM(lengths.shape, jnp.int32), pltpu.SemaphoreType.DMA],
        place, lengths, query, key, value, upstream, taps, rate, residue, skip,
    )


def features(spot, raw, masks, open_mask, end_mask, chain, taps, rate, decay, halo):
    tiles, states = raw.shape[0], rate.shape
    return call(
        feature_kernel, "features",
        [SMEM] + [VMEM] * 9,
        [(tiles, 3 * ROWS, LANES), (tiles, 5 * ROWS, LANES), states, states, (4, *states)],
        [],
        spot, raw, masks, open_mask, end_mask, chain, taps, rate, decay, halo,
    )


def segment_filter(spot, pre, *others):
    tiles = pre.shape[0]
    return call(
        segment_kernel, "segment_filter",
        [SMEM] + [VMEM] * (1 + len(others)),
        [(tiles, 2 * ROWS, LANES), (tiles, STEPS, LANES)],
        [(STEPS - 1, STEPS, SEGS, LANES)],
        spot, pre, *others,
    )


def local_filter(spot, pre, *others):
    tiles = pre.shape[0]
    return call(
        local_kernel, "local_filter",
        [SMEM] + [VMEM] * (1 + len(others)),
        [(tiles, 4 * ROWS, LANES), (tiles, MODES + 8, LANES)],
        [(2, SEGS, LANES), (MODES, LANES), (MODES, LANES)],
        spot, pre, *others,
    )


def filter_gradients(spot, raw, *others):
    tiles = raw.shape[0]
    half = (tiles // 2, REDUCED, LANES)
    return call(
        gradient_kernel, "filter_gradients",
        [SMEM] + [VMEM] * (1 + len(others)),
        [jax.ShapeDtypeStruct((ROWS, tiles * LANES), BF16), (tiles, 3 * ROWS, LANES), (24, tiles * LANES), half, half],
        [STAGE, pltpu.VMEM((ROWS, tiles * LANES), BF16), pltpu.SemaphoreType.DMA((CHUNKS,)), (2 * MODES, LANES)],
        spot, raw, *others, specs=[HBM] + [VMEM] * 4,
    )


def input_gradient(branch, gfeat, edge, taps, masks):
    [made] = call(
        partial(input_kernel, branch), "input_gradient",
        [VMEM] * 4,
        [jax.ShapeDtypeStruct((ROWS, taps.shape[2]), BF16)],
        [STAGE],
        gfeat, edge, taps, masks,
    )
    return made


def results(spot, kept, away):
    channels = 2 * kept.shape[0] * LANES
    shapes = (3, TAPS, channels), (MODES, channels), (1, channels)
    return call(
        result_kernel, "parameter_gradients",
        [SMEM, VMEM, VMEM], [jax.ShapeDtypeStruct(shape, F32) for shape in shapes], [], spot, kept, away,
    )


def combine(which, first, through, second):
    [made] = call(
        partial(combine_kernel, which), "combine", [VMEM] * 3, [first.shape], [], first, through, second
    )
    return made


def per_device(query_rows, key_rows, value_rows, cotangent, lengths, short_filter, residue, decay_rate, skip_gain):
    count = lax.axis_size("ctx")
    place = jnp.stack([lax.axis_index("ctx"), lax.axis_index("dp")]).astype(jnp.int32)
    spot = jnp.concatenate([place, lengths[0]])

    halo = lax.ppermute(tails(query_rows[0], key_rows[0], value_rows[0]), "ctx", [(i, i + 1) for i in range(count - 1)]).astype(F32)
    raw, masks, open_mask, end_mask, chain, taps, rate, residue, skip, decay = staged(
        place, lengths, query_rows[0], key_rows[0], value_rows[0], cotangent[0],
        short_filter, decay_rate.T, residue.T, skip_gain[None],
    )
    feat, pre, own, sent, through = features(spot, raw, masks, open_mask, end_mask, chain, taps, rate, decay, halo)

    pairs = [(i, i ^ 1) for i in range(count)]

    def onward(value, chips):
        moves = [(i, i + 2 * chips * (1 - 2 * (i % 2))) for i in range(count)]
        return lax.ppermute(value, "ctx", [(i, j) for i, j in moves if 0 <= j < count])

    chip_state = combine(1, lax.ppermute(sent, "ctx", pairs), through, own)
    chip_state, pre = lax.optimization_barrier((chip_state, pre))
    near_rows, paired = segment_filter(spot, pre, rate, decay, residue, skip)
    received, near_rows = lax.optimization_barrier((onward(chip_state, 1), near_rows))
    chip_state = combine(2, chip_state, through, received)
    chip_state, pre = lax.optimization_barrier((chip_state, pre))
    near, far = onward(chip_state, 1), onward(chip_state, 3)
    post, local = local_filter(spot, pre, paired, rate, decay, residue)
    far, post = lax.optimization_barrier((far, post))
    arrived, handed = call(
        arrive_kernel, "arrive", [VMEM] * 4, [own.shape, own.shape], [], near, far, own, through
    )
    handed = lax.ppermute(handed, "ctx", pairs)

    block_out, gfeat, edge, kept, away = filter_gradients(
        spot, raw, feat, near_rows, post, local, arrived, handed, own, sent, rate, decay, halo,
        masks, open_mask, end_mask,
    )

    def exchange(value, axis, flip):
        return lax.ppermute(value, axis, [(i, i ^ flip) for i in range(lax.axis_size(axis))])

    grad_inputs = []

    def exchanges(sent, axis, flips, beside):
        if beside == 0:
            return [exchange(value, axis, flip) for value, flip in zip(sent, flips)]
        *sent, edge_now = lax.optimization_barrier((*sent, next_edge))
        made = [input_gradient(len(grad_inputs) + i, gfeat, edge_now, taps, masks) for i in range(beside)]
        done = lax.optimization_barrier((*exchanges(sent, axis, flips, 0), *made))
        grad_inputs.extend(done[len(sent) :])
        return done[: len(sent)]

    total = kept + exchange(away, "ctx", 1)
    quarter = total.shape[0] // 4
    quarters = [total[quarter * i : quarter * (i + 1)] for i in range(4)]
    quarters[1], edge = lax.optimization_barrier((quarters[1], edge))
    next_edge = lax.ppermute(edge, "ctx", [(i, i - 1) for i in range(1, count)])
    one, two, three, next_edge = lax.optimization_barrier(
        (*exchanges(quarters[1:], "dp", (1, 2, 3), 0), next_edge)
    )
    total = (quarters[0] + one) + (two + three)
    total = total + exchange(total, "ctx", 2)
    one, two, three = exchanges([total] * 3, "ctx", (4, 8, 12), 2)
    total = (total + one) + (two + three)
    total = jnp.concatenate([total, *exchanges([total] * 3, "dp", (1, 2, 3), 1)])
    grad_short, grad_residue, grad_skip = results(spot, total, exchange(total, "ctx", 1))
    return (block_out[None], *(g[None] for g in grad_inputs), grad_short, grad_residue.T, grad_skip[0])


def solution(mesh):
    rows = P("dp", "ctx", "ch")
    return jax.shard_map(
        per_device,
        mesh=mesh,
        in_specs=(rows, rows, rows, rows, P("dp", None), P(None, None, "ch"), P("ch", None), P("ch", None), P("ch")),
        out_specs=(rows, rows, rows, rows, P(None, None, "ch"), P("ch", None), P("ch")),
        check_vma=False,
    )
```
